32 devices in a mesh: groups: 2 (over x), grid: 8 (over z, y), dp: 2 (over core).
Axes of the slice: x: 2, y: 2, z: 4, core: 2. Of those that a mesh axis runs over, the one named last changes fastest.
Arguments:
- acts: bfloat16 [4, 8, 192, 2560], P(('groups', 'dp'), 'grid'), parts along dimension 0, may hold values from -6 to 6
- cotangent: bfloat16 [4, 8, 192, 2560], P(('groups', 'dp'), 'grid'), parts along dimension 0, may hold values from -1.5 to 1.5
- w_gate: bfloat16 [8, 2560, 1792], P('grid'), may hold values from -0.078125 to 0.078125
- w_up: bfloat16 [8, 2560, 1792], P('grid'), may hold values from -0.078125 to 0.078125
- w_down: bfloat16 [8, 1792, 2560], P('grid'), may hold values from -0.0625 to 0.0625
Outputs:
- block_out: bfloat16 [4, 8, 192, 2560], P(('groups', 'dp'), 'grid'), parts along dimension 0
- input_grad: bfloat16 [4, 8, 192, 2560], P(('groups', 'dp'), 'grid'), parts along dimension 0
- gate_grad: bfloat16 [16, 2560, 1792], P(('groups', 'grid')), parts along dimension 0
- up_grad: bfloat16 [16, 2560, 1792], P(('groups', 'grid')), parts along dimension 0
- down_grad: bfloat16 [16, 1792, 2560], P(('groups', 'grid')), parts along dimension 0
The draws below stay inside these ranges and needn't reach their ends.
There are 2 independent parts, one for each index of `groups`. The reference program is written for one: setup_inputs(seed, part) draws one part's arguments, and reference() takes and returns one part's arrays. A program takes and returns all parts, laid end to end along the dimension named above; an argument that names none is the same for every part. Nothing has to cross between parts.
All inputs are finite; a program needn't handle non-finite values.
Results may differ from the reference program's by a relative error of at most 0.015.
Values may be sent and summed in bfloat16 or wider, within the bound.
No kernel may reach another device: no remote copies, remote signals or barrier semaphores. Data moves between devices by JAX's collectives and lax.ppermute only.
A program may use at most 192 MiB of HBM per device.

```python
import jax
import jax.numpy as jnp

D = 5120
FFW = 7168
TOK = 768
GC = 4
GR = 2
N_GRID = 8
N_DP = 2


def block_scale(own_key, shape, pieces, smallest, high):
    def one(dim, shards_of):
        heights = jax.random.uniform(jax.random.fold_in(jax.random.fold_in(own_key, 6), dim), (shards_of,), jnp.float32, smallest / len(pieces), high / len(pieces))
        return jnp.repeat(jnp.exp(heights), shape[dim] // shards_of).reshape((-1,) + (1,) * (len(shape) - dim - 1))

    level = one(*pieces[0])
    for cut in pieces[1:]:
        level = level * one(*cut)
    return level


def normal_values(key, extent, spread, limit, split=(), kind=jnp.bfloat16):
    entries = spread * jax.random.normal(key, extent, jnp.float32)
    if split:
        entries = entries * block_scale(key, extent, split, -0.22, 0.18)
    return jnp.clip(entries, -limit, limit).astype(kind)


def setup_inputs(seed: int = 0, part: int = 0) -> dict:
    key_of = jax.random.split(jax.random.key(seed), 6)
    part_keys = jax.random.split(jax.random.fold_in(key_of[5], part), 6)
    return {
        "acts": normal_values(part_keys[0], (N_DP, N_GRID, TOK // GC, D // GR), 1.0, 6.0, ((0, 2), (1, 8))),
        "cotangent": normal_values(part_keys[1], (N_DP, N_GRID, TOK // GC, D // GR), 0.25, 1.5, ((0, 2), (1, 8))),
        "w_gate": normal_values(key_of[2], (N_GRID, D // GR, FFW // GC), D ** -0.5, 0.078125, ((0, 8),)),
        "w_up": normal_values(key_of[3], (N_GRID, D // GR, FFW // GC), D ** -0.5, 0.078125, ((0, 8),)),
        "w_down": normal_values(key_of[4], (N_GRID, FFW // GC, D // GR), FFW ** -0.5, 0.0625, ((0, 8),)),
    }


def to_rows(tiles):
    blocks = tiles.reshape(N_DP, GR, GC, TOK // GC, D // GR)
    return blocks.transpose(0, 2, 3, 1, 4).reshape(N_DP * TOK, D)


def to_tiles(rows_all):
    blocks = rows_all.reshape(N_DP, GC, TOK // GC, GR, D // GR)
    return blocks.transpose(0, 3, 1, 2, 4).reshape(N_DP, GR * GC, TOK // GC, D // GR)


def weight_rows(tiles):
    return tiles.reshape(GR, GC, D // GR, FFW // GC).transpose(0, 2, 1, 3).reshape(D, FFW)


def weight_tiles(full):
    return full.reshape(GR, D // GR, GC, FFW // GC).transpose(0, 2, 1, 3).reshape(GR * GC, D // GR, FFW // GC)


def down_rows(tiles):
    return tiles.reshape(GR, GC, FFW // GC, D // GR).transpose(1, 2, 0, 3).reshape(FFW, D)


def down_tiles(full):
    return full.reshape(GC, FFW // GC, GR, D // GR).transpose(2, 0, 1, 3).reshape(GR * GC, FFW // GC, D // GR)


def reference(acts, cotangent, w_gate, w_up, w_down):
    inputs = to_rows(acts)
    out_grads = to_rows(cotangent)
    gate_full = weight_rows(w_gate)
    up_full = weight_rows(w_up)
    down_full = down_rows(w_down)
    gate_pre = jnp.dot(inputs, gate_full, preferred_element_type=jnp.float32)
    up_proj = jnp.dot(inputs, up_full, preferred_element_type=jnp.float32)
    sigmoid_g = jax.nn.sigmoid(gate_pre)
    activated = gate_pre * sigmoid_g
    hidden = (activated * up_proj).astype(jnp.bfloat16)
    block_out = (inputs.astype(jnp.float32) + jnp.dot(hidden, down_full, preferred_element_type=jnp.float32)).astype(jnp.bfloat16)
    hidden_grad = jnp.dot(out_grads, down_full.T, preferred_element_type=jnp.float32)
    gate_back = (hidden_grad * up_proj * sigmoid_g * (1.0 + gate_pre * (1.0 - sigmoid_g))).astype(jnp.bfloat16)
    up_back = (hidden_grad * activated).astype(jnp.bfloat16)
    input_sum = jnp.dot(gate_back, gate_full.T, preferred_element_type=jnp.float32) + jnp.dot(up_back, up_full.T, preferred_element_type=jnp.float32)
    input_grad = (out_grads.astype(jnp.float32) + input_sum).astype(jnp.bfloat16)
    gate_grad = jnp.dot(inputs.T, gate_back, preferred_element_type=jnp.float32).astype(jnp.bfloat16)
    up_grad = jnp.dot(inputs.T, up_back, preferred_element_type=jnp.float32).astype(jnp.bfloat16)
    down_grad = jnp.dot(hidden.T, out_grads, preferred_element_type=jnp.float32).astype(jnp.bfloat16)
    return (to_tiles(block_out), to_tiles(input_grad), weight_tiles(gate_grad), weight_tiles(up_grad), down_tiles(down_grad))
```

```python
import functools

import jax
import jax.numpy as jnp
from jax import lax
from jax.experimental import pallas as pl
from jax.experimental.pallas import tpu as pltpu
from jax.sharding import PartitionSpec as P

VMEM_BYTES = 62 * 1024 * 1024
TILE = 256
COST_SCALE = 0.03e9
G, U, PRE = 0, 1, 2


def from_partner(block, axis, stride):
    count = lax.axis_size(axis)
    route = []
    for low in range(count):
        high = low | 1 << stride
        if high != low and high < count:
            route += [(low, high), (high, low)]
    return lax.ppermute(block, axis, route)


def contract_rows(left, right):
    return lax.dot_general(
        left, right, (((0,), (0,)), ((), ())), preferred_element_type=jnp.float32
    )


def contract_cols(left, right):
    return lax.dot_general(
        left, right, (((1,), (1,)), ((), ())), preferred_element_type=jnp.float32
    )


def order_pair(is_upper, mine, other, dim=1):
    return jnp.where(
        is_upper, jnp.concatenate([other, mine], dim), jnp.concatenate([mine, other], dim)
    )


def column_sum(partial_term, total_rows, col_bits, row_bits, my_row):
    result_sum = partial_term(0, total_rows)
    for level_bit in range(row_bits - 1, -1, -1):
        half_rows = result_sum.shape[1] // 2
        lower_half = result_sum[:, :half_rows]
        upper_half = result_sum[:, half_rows:]
        is_upper = my_row >> level_bit & 1 == 1
        kept_half = jnp.where(is_upper, upper_half, lower_half)
        given_half = jnp.where(is_upper, lower_half, upper_half)
        result_sum = kept_half + from_partner(
            given_half.astype(jnp.bfloat16), "grid", col_bits + level_bit
        ).astype(given_half.dtype)
    return result_sum


def column_gather(pieces, col_bits, row_bits, my_row):
    for level_bit in range(row_bits):
        partner = from_partner(pieces, "grid", col_bits + level_bit)
        pieces = order_pair(my_row >> level_bit & 1 == 1, pieces, partner)
    return pieces


def row_sum(full_sum, col_bits, my_col):
    for level_bit in range(col_bits - 1, -1, -1):
        half_rows = full_sum.shape[0] // 2
        lower_half = full_sum[:half_rows]
        upper_half = full_sum[half_rows:]
        is_upper = my_col >> level_bit & 1 == 1
        kept_half = jnp.where(is_upper, upper_half, lower_half)
        given_half = jnp.where(is_upper, lower_half, upper_half)
        full_sum = kept_half + from_partner(
            given_half.astype(jnp.bfloat16), "grid", level_bit
        ).astype(given_half.dtype)
    return full_sum


def any_grid(acts, cotangent, w_gate, w_up, w_down):
    grid_size = lax.axis_size("grid")
    grid_cols = min(8, grid_size // 2)
    grid_rows = grid_size // grid_cols
    col_bits = grid_cols.bit_length() - 1
    row_bits = grid_rows.bit_length() - 1
    position = lax.axis_index("grid")
    my_row = position // grid_cols
    my_col = position % grid_cols
    own_acts = acts[0, 0]
    own_grads = cotangent[0, 0]
    gate_tile = w_gate[0]
    up_tile = w_up[0]
    down_tile = w_down[0]
    gathered = jnp.stack([own_acts, own_grads])
    for level_bit in range(col_bits):
        partner = from_partner(gathered, "grid", level_bit)
        gathered = order_pair(my_col >> level_bit & 1 == 1, gathered, partner)
    inputs_row = gathered[0]
    out_grad_row = gathered[1]
    total_rows = inputs_row.shape[0]

    def gate_up_term(row_start, row_count):
        return jnp.stack(
            [
                jnp.dot(inputs_row, gate_tile, preferred_element_type=jnp.float32),
                jnp.dot(inputs_row, up_tile, preferred_element_type=jnp.float32),
            ]
        )

    summed = column_sum(gate_up_term, total_rows, col_bits, row_bits, my_row)
    gate_pre = summed[0]
    up_proj = summed[1]
    sigmoid_g = jax.nn.sigmoid(gate_pre)
    activated = gate_pre * sigmoid_g
    hidden = (activated * up_proj).astype(jnp.bfloat16)
    hidden_full = column_gather(hidden[None], col_bits, row_bits, my_row)[0]
    output_sum = row_sum(
        jnp.dot(hidden_full, down_tile, preferred_element_type=jnp.float32), col_bits, my_col
    )
    block_out = (own_acts.astype(jnp.float32) + output_sum).astype(jnp.bfloat16)

    def hidden_grad_term(row_start, row_count):
        return contract_cols(out_grad_row, down_tile)[None]

    hidden_grad = column_sum(hidden_grad_term, total_rows, col_bits, row_bits, my_row)[0]
    gate_back = (hidden_grad * up_proj * sigmoid_g * (1.0 + gate_pre * (1.0 - sigmoid_g))).astype(
        jnp.bfloat16
    )
    up_back = (hidden_grad * activated).astype(jnp.bfloat16)
    backs_full = column_gather(jnp.stack([gate_back, up_back]), col_bits, row_bits, my_row)
    down_local = contract_rows(hidden_full, out_grad_row)
    input_part = contract_cols(backs_full[0], gate_tile) + contract_cols(backs_full[1], up_tile)
    input_sum = row_sum(input_part, col_bits, my_col)
    input_grad = (own_grads.astype(jnp.float32) + input_sum).astype(jnp.bfloat16)
    gate_local = contract_rows(inputs_row, backs_full[0])
    up_local = contract_rows(inputs_row, backs_full[1])
    gate_total, up_total, down_total = (
        lax.psum(gate_local.astype(jnp.bfloat16), "dp").astype(jnp.float32),
        lax.psum(up_local.astype(jnp.bfloat16), "dp").astype(jnp.float32),
        lax.psum(down_local.astype(jnp.bfloat16), "dp").astype(jnp.float32),
    )
    return (
        block_out[None, None],
        input_grad[None, None],
        gate_total.astype(jnp.bfloat16)[None],
        up_total.astype(jnp.bfloat16)[None],
        down_total.astype(jnp.bfloat16)[None],
    )


class Order:
    def __init__(self):
        self.token = None
        self.calls = 0
        self.due = []

    def need(self, array, calls):
        self.due.append((self.calls + calls, array))
        return array

    def call(self, body, name, cost, steps, inputs, outputs, scratch=(), after=(), aliases=()):
        after = list(after) + ([] if self.token is None else [self.token])
        after += [array for call, array in self.due if call <= self.calls]
        self.due = [(call, array) for call, array in self.due if call > self.calls]
        self.calls += 1
        n_in, n_after, n_out = len(inputs), len(after), len(outputs)

        def kernel(*refs):
            ins = refs[:n_in]
            outs = refs[n_in + n_after : n_in + n_after + n_out]
            refs[n_in + n_after + n_out][...] = jnp.zeros((8, 128), jnp.float32)
            body(ins, outs, refs[n_in + n_after + n_out + 1 :])

        *results, self.token = pl.pallas_call(
            kernel,
            name=name,
            grid=(steps,),
            in_specs=[spec for _, spec in inputs]
            + [pl.BlockSpec(memory_space=pl.ANY) for _ in after],
            out_specs=[spec for _, spec in outputs] + [pl.BlockSpec((8, 128), lambda j: (0, 0))],
            out_shape=[shape for shape, _ in outputs]
            + [jax.ShapeDtypeStruct((8, 128), jnp.float32)],
            scratch_shapes=list(scratch),
            input_output_aliases=dict(aliases),
            cost_estimate=pl.CostEstimate(
                flops=int(cost * COST_SCALE), bytes_accessed=0, transcendentals=0
            ),
            compiler_params=pltpu.CompilerParams(vmem_limit_bytes=VMEM_BYTES),
        )(*[array for array, _ in inputs], *after)
        return results

    def hold(self, array, after):
        inputs = [(array, pl.BlockSpec(memory_space=pl.ANY))]
        outputs = [(jax.ShapeDtypeStruct(array.shape, array.dtype), inputs[0][1])]
        return self.call(
            lambda *_: None, "hold", 0.6, 1, inputs, outputs, after=after, aliases={0: 0}.items()
        )[0]


def weight_specs(weights, kinds, first):
    gate, up, down = weights
    depth = gate.shape[1]
    wide = pl.BlockSpec((1, depth, TILE), lambda j: (0, 0, first + j))
    tall = pl.BlockSpec((1, TILE, depth), lambda j: (0, first + j, 0))
    return [((gate, up, down)[kind], tall if kind == PRE else wide) for kind in kinds]


def partials(order, units, tiles, sources, weights, after=()):
    first, count = tiles
    rows, depth = sources[0].shape[2:]
    kinds = [kind for kind in (G, U, PRE) if any(kind in unit[0] for unit in units)]
    token_spec = pl.BlockSpec((1, 1, rows, depth), lambda j: (0, 0, 0, 0))
    inputs = [(sources[kind == PRE], token_spec) for kind in kinds]
    inputs += weight_specs(weights, kinds, first)
    n = len(kinds)

    def body(ins, outs, _):
        for i, kind in enumerate(kinds):
            left, right = ins[i][0, 0], ins[n + i][0]
            if kind == PRE:
                term = contract_cols(left, right)
            else:
                term = jnp.dot(left, right, preferred_element_type=jnp.float32)
            for m, (unit_kinds, start, size) in enumerate(units):
                if kind in unit_kinds:
                    at = unit_kinds.index(kind)
                    outs[2 * m][at] = term[start : start + size]
                    outs[2 * m + 1][at] = term[start : start + size].astype(jnp.bfloat16)

    outputs = []
    for unit_kinds, _, size in units:
        shape = (len(unit_kinds), size, count * TILE)
        spec = pl.BlockSpec((len(unit_kinds), size, TILE), lambda j: (0, 0, j))
        outputs.append((jax.ShapeDtypeStruct(shape, jnp.float32), spec))
        outputs.append((jax.ShapeDtypeStruct(shape, jnp.bfloat16), spec))
    results = order.call(body, "partials", (1 + 0.8 * count) * n, count, inputs, outputs, after=after)
    return list(zip(results[::2], results[1::2]))


def hidden_and_back(order, tiles, parts, weights, out_type, addend=()):
    first, count = tiles
    sizes = [kept.shape[1] for kept, _ in parts]
    rows = sum(sizes)
    depth = weights[0].shape[1]
    inputs = []
    for pair, size in zip(parts, sizes):
        spec = pl.BlockSpec((3, size, TILE), lambda j: (0, 0, j))
        inputs += [(array, spec) for array in pair]
    n = len(inputs)
    inputs += weight_specs(weights, (G, U, PRE), first)
    sums_spec = pl.BlockSpec((rows, depth), lambda j: (0, 0))
    inputs += [(array, sums_spec) for array in addend]

    def body(ins, outs, scratch):
        wg_ref, wu_ref, wd_ref = ins[n : n + 3]
        hqr_ref = outs[0]
        acc_ref = scratch[0]
        j = pl.program_id(0)
        terms = [ins[m][...] + ins[m + 1][...].astype(jnp.float32) for m in range(0, n, 2)]
        g, u, p = terms[0] if len(terms) == 1 else jnp.concatenate(terms, 1)
        s = jax.nn.sigmoid(g)
        a = g * s
        h = (a * u).astype(jnp.bfloat16)
        q = (p * u * s * (1.0 + g * (1.0 - s))).astype(jnp.bfloat16)
        r = (p * a).astype(jnp.bfloat16)
        for i, value in enumerate((h, q, r)):
            hqr_ref[0, i] = value
            hqr_ref[1, i] = value
        out_term = jnp.dot(h, wd_ref[0], preferred_element_type=jnp.float32)
        in_term = contract_cols(q, wg_ref[0]) + contract_cols(r, wu_ref[0])

        @pl.when(j == 0)
        def _():
            acc_ref[0] = out_term
            acc_ref[1] = in_term

        @pl.when(j > 0)
        def _():
            acc_ref[0] += out_term
            acc_ref[1] += in_term

        @pl.when(j == count - 1)
        def _():
            for i in range(2):
                total = acc_ref[i]
                if addend:
                    total = total + ins[n + 3 + i][...].astype(jnp.float32)
                outs[1 + i][...] = total.astype(out_type)

    outputs = [
        (
            jax.ShapeDtypeStruct((2, 3, rows, count * TILE), jnp.bfloat16),
            pl.BlockSpec((2, 3, rows, TILE), lambda j: (0, 0, 0, j)),
        ),
    ]
    outputs += [(jax.ShapeDtypeStruct((rows, depth), out_type), sums_spec)] * 2
    scratch = [pltpu.VMEM((2, rows, depth), jnp.float32)]
    return order.call(body, "hidden_and_back", 3 + 2.2 * count, count, inputs, outputs, scratch)


def assemble(order, blocks):
    rows, depth = blocks[0].shape[2:]
    total = 2 * rows * len(blocks)
    inputs = []
    for block in blocks:
        for part in range(2):
            index = functools.partial(lambda j, part: (0, part, 0, j), part=part)
            inputs.append((block, pl.BlockSpec((2, 1, rows, TILE), index)))

    def body(ins, outs, scratch):
        xt_ref, e_ref = outs
        x_all = scratch[0]
        for b in range(len(blocks)):
            for d in range(2):
                at = pl.ds((2 * b + d) * rows, rows)
                x_all[at, :] = ins[2 * b][d, 0]
                e_ref[at, :] = ins[2 * b + 1][d, 0]
        xt_ref[...] = x_all[...].T

    outputs = [
        (
            jax.ShapeDtypeStruct((depth, total), jnp.bfloat16),
            pl.BlockSpec((TILE, total), lambda j: (j, 0)),
        ),
        (
            jax.ShapeDtypeStruct((total, depth), jnp.bfloat16),
            pl.BlockSpec((total, TILE), lambda j: (0, j)),
        ),
    ]
    scratch = [pltpu.VMEM((total, TILE), jnp.bfloat16)]
    return order.call(body, "assemble", 10, depth // TILE, inputs, outputs, scratch)


def weight_grads(order, tiles, tokens, pieces, width, so_far=None, into=None):
    first, count = tiles
    xt, e_all = tokens
    depth, total = xt.shape
    whole = [
        pl.BlockSpec((depth, total), lambda j: (0, 0), pipeline_mode=pl.Buffered(1)),
        pl.BlockSpec((total, depth), lambda j: (0, 0), pipeline_mode=pl.Buffered(1)),
    ]
    inputs = [(xt, whole[0]), (e_all, whole[1])]
    for _, _, hqr, start in pieces:
        index = functools.partial(lambda j, start: (0, 0, 0, start + j), start=start)
        inputs.append((hqr, pl.BlockSpec((2, 3, hqr.shape[2], TILE), index)))
    wide = pl.BlockSpec((1, depth, TILE), lambda j: (0, 0, first + j))
    tall = pl.BlockSpec((1, TILE, depth), lambda j: (0, first + j, 0))
    specs = (wide, wide, tall)
    n = len(inputs)
    if so_far is not None:
        inputs += list(zip(so_far, specs))
    aliases = {}
    if into is not None:
        for i, array in enumerate(into):
            aliases[len(inputs)] = i
            inputs.append((array, pl.BlockSpec(memory_space=pl.ANY)))

    def body(ins, outs, scratch):
        hqr_all = scratch[0]
        for m, (*starts, hqr, _) in enumerate(pieces):
            for d, start in enumerate(starts):
                for i in range(3):
                    hqr_all[i, start : start + hqr.shape[2], :] = ins[2 + m][d, i]
        terms = (
            lambda: jnp.dot(ins[0][...], hqr_all[1], preferred_element_type=jnp.float32),
            lambda: jnp.dot(ins[0][...], hqr_all[2], preferred_element_type=jnp.float32),
            lambda: contract_rows(hqr_all[0], ins[1][...]),
        )
        for i, term in enumerate(terms):
            value = term()
            if so_far is not None:
                value = value + ins[n + i][0].astype(jnp.float32)
            outs[i][0] = value.astype(jnp.bfloat16)

    shapes = ((1, depth, width), (1, depth, width), (1, width, depth))
    outputs = [
        (jax.ShapeDtypeStruct(shape, jnp.bfloat16), spec) for shape, spec in zip(shapes, specs)
    ]
    scratch = [pltpu.VMEM((3, total, TILE), jnp.bfloat16)]
    return order.call(
        body, "weight_grads", 4 + 4 * count, count, inputs, outputs, scratch, aliases=aliases.items()
    )


def add_row_sums(order, own_sums, near_sums, far_sums, acts, cotangent):
    rows, depth = acts.shape[2:]
    step = rows // 4
    spec = pl.BlockSpec((step, depth), lambda j: (j, 0))
    token_spec = pl.BlockSpec((1, 1, step, depth), lambda j: (0, 0, j, 0))
    inputs = [(array, spec) for array in (*own_sums, *near_sums, *far_sums)]
    inputs += [(acts, token_spec), (cotangent, token_spec)]

    def body(ins, outs, _):
        for i in range(2):
            total = ins[i][...] + ins[2 + i][...].astype(jnp.float32)
            total += ins[4 + i][...].astype(jnp.float32) + ins[6 + i][0, 0].astype(jnp.float32)
            outs[i][0, 0] = total.astype(jnp.bfloat16)

    outputs = [(jax.ShapeDtypeStruct(acts.shape, jnp.bfloat16), token_spec)] * 2
    return order.call(body, "add_row_sums", 5, 4, inputs, outputs)


def two_by_four(acts, cotangent, w_gate, w_up, w_down):
    near, far, across = 0, 1, 2
    rows = acts.shape[2]
    half = rows // 2
    width = w_gate.shape[2]
    n_tiles = width // TILE
    weights = (w_gate, w_up, w_down)
    order = Order()

    sources = {"own": (acts, cotangent)}

    def gather(block, origin, bit):
        sources[block] = tuple(from_partner(array, "grid", bit) for array in sources[origin])

    gather("near", "own", near)
    gather("far", "own", far)

    a = max(1, n_tiles * 3 // 7)
    b = n_tiles - 1
    every = (0, n_tiles)
    chunks = {"c0": (0, a), "c1": (a, b - a), "c2": (b, n_tiles - b)}
    own, ready, got = {}, {}, {}

    def compute(names, units, tiles, block, after=()):
        after = [got[key] for key in after]
        results = partials(order, units, tiles, sources[block], weights, after)
        for name, (kept, rounded) in zip(names, results):
            own[name], ready[name] = kept, rounded

    def send(name, after=()):
        rounded = ready[name]
        if after:
            rounded = order.hold(rounded, [got[key] for key in after])
        got[name] = from_partner(rounded, "grid", across)

    hqr, sums, passed = {}, {}, {}

    def both_replicas(pair):
        return lax.all_to_all(pair, "dp", 0, 0, tiled=True)

    def twice(x, e):
        return jnp.stack([x[0, 0], e[0, 0], x[0, 0], e[0, 0]]).reshape(2, 2, *x.shape[2:])

    def finish(name, names, tiles, out_type=jnp.bfloat16, addend=()):
        parts = [(own[key], got[key]) for key in names]
        pair, *sums[name] = hidden_and_back(order, tiles, parts, weights, out_type, addend)
        hqr[name] = both_replicas(pair)

    def pieces_of(groups, start):
        found = []
        at = 0
        for group in groups:
            size = sum(hqr[name].shape[2] for name in group)
            for name in group:
                first = start if hqr[name].shape[3] == width else 0
                found.append((at, at + size, hqr[name], first))
                at += hqr[name].shape[2]
            at += size
        return found

    def pass_on(name, bit, calls):
        passed[name] = [order.need(from_partner(sum, "grid", bit), calls) for sum in sums[name]]

    def collect(*names):
        return assemble(order, [both_replicas(twice(*sources[name])) for name in names])

    gup = (G, U, PRE)
    everything = [(gup, 0, rows)]
    halves = [(gup, 0, half), (gup, half, half)]
    compute(["c0"], everything, chunks["c0"], "own")
    send("c0")
    compute(["c1"], everything, chunks["c1"], "own")
    compute(["c2"], everything, chunks["c2"], "own")
    compute(["na", "nb"], halves, every, "near")
    send("na")
    send("nb", ["c0"])
    finish("c0", ["c0"], chunks["c0"], jnp.float32)
    sources["far"] = tuple(order.hold(array, []) for array in sources["far"])
    gather("both", "far", near)
    compute(["fa", "fb"], halves, every, "far")
    late = collect("far", "own")
    compute(["ba", "bb"], halves, every, "both", ["na"])
    send("ba")
    send("bb", ["nb"])
    finish("near", ["na", "nb"], every)
    pass_on("near", near, 3)
    early = collect("near", "both")
    send("fa", ["ba"])
    send("fb", ["bb"])
    finish("both", ["ba", "bb"], every)
    pass_on("both", near, 9)
    early_pieces = pieces_of([["near"], ["both"]], 0)
    mid = n_tiles // 2
    first = weight_grads(order, (0, mid), early, early_pieces, width)
    send("c1", ["fa"])
    first = weight_grads(
        order,
        (mid, n_tiles - mid),
        early,
        pieces_of([["near"], ["both"]], mid),
        width,
        into=first,
    )
    send("c2", ["fb"])
    finish("far", ["fa", "fb"], every, addend=passed["both"])
    pass_on("far", far, 20)

    grads = None

    def final(name):
        return weight_grads(
            order,
            chunks[name],
            late,
            pieces_of([["far"], [name]], chunks[name][0]),
            width,
            first,
            grads,
        )

    grads = final("c0")
    last = "c0"
    for name in ("c1", "c2"):
        finish(name, [name], chunks[name], jnp.float32, sums[last])
        last = name
        grads = final(name)
    outs = add_row_sums(order, sums[last], passed["near"], passed["far"], acts, cotangent)
    return (*outs, *grads)


def per_device(acts, cotangent, w_gate, w_up, w_down):
    fits = acts.shape[2] % 64 == 0 and acts.shape[3] % TILE == 0 and w_gate.shape[2] % TILE == 0
    if lax.axis_size("grid") == 8 and lax.axis_size("dp") == 2 and fits:
        return two_by_four(acts, cotangent, w_gate, w_up, w_down)
    return any_grid(acts, cotangent, w_gate, w_up, w_down)


def solution(mesh):
    return jax.shard_map(
        per_device,
        mesh=mesh,
        in_specs=(
            P(("groups", "dp"), "grid", None, None),
            P(("groups", "dp"), "grid", None, None),
            P("grid", None, None),
            P("grid", None, None),
            P("grid", None, None),
        ),
        out_specs=(
            P(("groups", "dp"), "grid", None, None),
            P(("groups", "dp"), "grid", None, None),
            P(("groups", "grid"), None, None),
            P(("groups", "grid"), None, None),
            P(("groups", "grid"), None, None),
        ),
        check_vma=False,
    )
```

```python
import functools
import itertools

import jax
import jax.numpy as jnp
from jax import lax
from jax.experimental import pallas as pl
from jax.experimental.pallas import tpu as pltpu
from jax.sharding import PartitionSpec as P

VMEM_BYTES = 62 * 1024 * 1024
TILE = 256
COST_SCALE = 0.1e9
G, U, PRE = 0, 1, 2


def from_partner(block, axis, stride):
    count = lax.axis_size(axis)
    route = []
    for low in range(count):
        high = low | 1 << stride
        if high != low and high < count:
            route += [(low, high), (high, low)]
    return lax.ppermute(block, axis, route)


def contract_rows(left, right):
    return lax.dot_general(
        left, right, (((0,), (0,)), ((), ())), preferred_element_type=jnp.float32
    )


def contract_cols(left, right):
    return lax.dot_general(
        left, right, (((1,), (1,)), ((), ())), preferred_element_type=jnp.float32
    )


def order_pair(is_upper, mine, other, dim=1):
    return jnp.where(
        is_upper, jnp.concatenate([other, mine], dim), jnp.concatenate([mine, other], dim)
    )


def column_sum(partial_term, total_rows, col_bits, row_bits, my_row):
    result_sum = partial_term(0, total_rows)
    for level_bit in range(row_bits - 1, -1, -1):
        half_rows = result_sum.shape[1] // 2
        lower_half = result_sum[:, :half_rows]
        upper_half = result_sum[:, half_rows:]
        is_upper = my_row >> level_bit & 1 == 1
        kept_half = jnp.where(is_upper, upper_half, lower_half)
        given_half = jnp.where(is_upper, lower_half, upper_half)
        result_sum = kept_half + from_partner(
            given_half.astype(jnp.bfloat16), "grid", col_bits + level_bit
        ).astype(given_half.dtype)
    return result_sum


def column_gather(pieces, col_bits, row_bits, my_row):
    for level_bit in range(row_bits):
        partner = from_partner(pieces, "grid", col_bits + level_bit)
        pieces = order_pair(my_row >> level_bit & 1 == 1, pieces, partner)
    return pieces


def row_sum(full_sum, col_bits, my_col):
    for level_bit in range(col_bits - 1, -1, -1):
        half_rows = full_sum.shape[0] // 2
        lower_half = full_sum[:half_rows]
        upper_half = full_sum[half_rows:]
        is_upper = my_col >> level_bit & 1 == 1
        kept_half = jnp.where(is_upper, upper_half, lower_half)
        given_half = jnp.where(is_upper, lower_half, upper_half)
        full_sum = kept_half + from_partner(
            given_half.astype(jnp.bfloat16), "grid", level_bit
        ).astype(given_half.dtype)
    return full_sum


def any_grid(acts, cotangent, w_gate, w_up, w_down):
    grid_size = lax.axis_size("grid")
    grid_cols = min(8, grid_size // 2)
    grid_rows = grid_size // grid_cols
    col_bits = grid_cols.bit_length() - 1
    row_bits = grid_rows.bit_length() - 1
    position = lax.axis_index("grid")
    my_row = position // grid_cols
    my_col = position % grid_cols
    own_acts = acts[0, 0]
    own_grads = cotangent[0, 0]
    gate_tile = w_gate[0]
    up_tile = w_up[0]
    down_tile = w_down[0]
    gathered = jnp.stack([own_acts, own_grads])
    for level_bit in range(col_bits):
        partner = from_partner(gathered, "grid", level_bit)
        gathered = order_pair(my_col >> level_bit & 1 == 1, gathered, partner)
    inputs_row = gathered[0]
    out_grad_row = gathered[1]
    total_rows = inputs_row.shape[0]

    def gate_up_term(row_start, row_count):
        return jnp.stack(
            [
                jnp.dot(inputs_row, gate_tile, preferred_element_type=jnp.float32),
                jnp.dot(inputs_row, up_tile, preferred_element_type=jnp.float32),
            ]
        )

    summed = column_sum(gate_up_term, total_rows, col_bits, row_bits, my_row)
    gate_pre = summed[0]
    up_proj = summed[1]
    sigmoid_g = jax.nn.sigmoid(gate_pre)
    activated = gate_pre * sigmoid_g
    hidden = (activated * up_proj).astype(jnp.bfloat16)
    hidden_full = column_gather(hidden[None], col_bits, row_bits, my_row)[0]
    output_sum = row_sum(
        jnp.dot(hidden_full, down_tile, preferred_element_type=jnp.float32), col_bits, my_col
    )
    block_out = (own_acts.astype(jnp.float32) + output_sum).astype(jnp.bfloat16)

    def hidden_grad_term(row_start, row_count):
        return contract_cols(out_grad_row, down_tile)[None]

    hidden_grad = column_sum(hidden_grad_term, total_rows, col_bits, row_bits, my_row)[0]
    gate_back = (hidden_grad * up_proj * sigmoid_g * (1.0 + gate_pre * (1.0 - sigmoid_g))).astype(
        jnp.bfloat16
    )
    up_back = (hidden_grad * activated).astype(jnp.bfloat16)
    backs_full = column_gather(jnp.stack([gate_back, up_back]), col_bits, row_bits, my_row)
    down_local = contract_rows(hidden_full, out_grad_row)
    input_part = contract_cols(backs_full[0], gate_tile) + contract_cols(backs_full[1], up_tile)
    input_sum = row_sum(input_part, col_bits, my_col)
    input_grad = (own_grads.astype(jnp.float32) + input_sum).astype(jnp.bfloat16)
    gate_local = contract_rows(inputs_row, backs_full[0])
    up_local = contract_rows(inputs_row, backs_full[1])
    gate_total, up_total, down_total = (
        lax.psum(gate_local.astype(jnp.bfloat16), "dp").astype(jnp.float32),
        lax.psum(up_local.astype(jnp.bfloat16), "dp").astype(jnp.float32),
        lax.psum(down_local.astype(jnp.bfloat16), "dp").astype(jnp.float32),
    )
    return (
        block_out[None, None],
        input_grad[None, None],
        gate_total.astype(jnp.bfloat16)[None],
        up_total.astype(jnp.bfloat16)[None],
        down_total.astype(jnp.bfloat16)[None],
    )


class Order:
    def __init__(self):
        self.token = None
        self.calls = 0
        self.due = []

    def need(self, array, calls):
        self.due.append((self.calls + calls, array))
        return array

    def call(self, body, name, cost, steps, inputs, outputs, scratch=(), after=(), aliases=()):
        after = list(after) + ([] if self.token is None else [self.token])
        after += [array for call, array in self.due if call <= self.calls]
        self.due = [(call, array) for call, array in self.due if call > self.calls]
        self.calls += 1
        n_in, n_after, n_out = len(inputs), len(after), len(outputs)

        def kernel(*refs):
            ins = refs[:n_in]
            outs = refs[n_in + n_after : n_in + n_after + n_out]
            refs[n_in + n_after + n_out][...] = jnp.zeros((8, 128), jnp.float32)
            body(ins, outs, refs[n_in + n_after + n_out + 1 :])

        *results, self.token = pl.pallas_call(
            kernel,
            name=name,
            grid=(steps,),
            in_specs=[spec for _, spec in inputs]
            + [pl.BlockSpec(memory_space=pl.ANY) for _ in after],
            out_specs=[spec for _, spec in outputs] + [pl.BlockSpec((8, 128), lambda j: (0, 0))],
            out_shape=[shape for shape, _ in outputs]
            + [jax.ShapeDtypeStruct((8, 128), jnp.float32)],
            scratch_shapes=list(scratch),
            input_output_aliases=dict(aliases),
            cost_estimate=pl.CostEstimate(
                flops=int(cost * COST_SCALE), bytes_accessed=0, transcendentals=0
            ),
            compiler_params=pltpu.CompilerParams(vmem_limit_bytes=VMEM_BYTES),
        )(*[array for array, _ in inputs], *after)
        return results

    def hold(self, array, after):
        inputs = [(array, pl.BlockSpec(memory_space=pl.ANY))]
        outputs = [(jax.ShapeDtypeStruct(array.shape, array.dtype), inputs[0][1])]
        return self.call(
            lambda *_: None, "hold", 0.6, 1, inputs, outputs, after=after, aliases={0: 0}.items()
        )[0]


def weight_specs(weights, kinds, first):
    gate, up, down = weights
    depth = gate.shape[1]
    wide = pl.BlockSpec((1, depth, TILE), lambda j: (0, 0, first + j))
    tall = pl.BlockSpec((1, TILE, depth), lambda j: (0, first + j, 0))
    return [((gate, up, down)[kind], tall if kind == PRE else wide) for kind in kinds]


def partials(order, units, tiles, sources, weights, after=(), pack=False):
    first, count = tiles
    rows, depth = sources[0].shape[2:]
    kinds = [kind for kind in (G, U, PRE) if any(kind in unit[0] for unit in units)]
    token_spec = pl.BlockSpec((1, 1, rows, depth), lambda j: (0, 0, 0, 0))
    inputs = [(sources[kind == PRE], token_spec) for kind in kinds]
    inputs += weight_specs(weights, kinds, first)
    n = len(kinds)

    def body(ins, outs, _):
        for i, kind in enumerate(kinds):
            left, right = ins[i][0, 0], ins[n + i][0]
            if kind == PRE:
                term = contract_cols(left, right)
            else:
                term = jnp.dot(left, right, preferred_element_type=jnp.float32)
            for m, (unit_kinds, start, size) in enumerate(units):
                if kind in unit_kinds:
                    at = unit_kinds.index(kind)
                    outs[2 * m][at] = term[start : start + size]
                    outs[2 * m + 1][at] = term[start : start + size].astype(jnp.bfloat16)
        if pack:

            @pl.when(pl.program_id(0) == 0)
            def _():
                for d in range(2):
                    outs[-1][d, 0] = ins[kinds.index(G)][0, 0]
                    outs[-1][d, 1] = ins[kinds.index(PRE)][0, 0]

    outputs = []
    for unit_kinds, _, size in units:
        shape = (len(unit_kinds), size, count * TILE)
        spec = pl.BlockSpec((len(unit_kinds), size, TILE), lambda j: (0, 0, j))
        outputs.append((jax.ShapeDtypeStruct(shape, jnp.float32), spec))
        outputs.append((jax.ShapeDtypeStruct(shape, jnp.bfloat16), spec))
    if pack:
        shape = (2, 2, rows, depth)
        spec = pl.BlockSpec(shape, lambda j: (0, 0, 0, 0))
        outputs.append((jax.ShapeDtypeStruct(shape, jnp.bfloat16), spec))
    cost = (1 + 0.8 * count) * n
    results = order.call(body, "partials", cost, count, inputs, outputs, after=after)
    pairs = list(zip(results[: 2 * len(units) : 2], results[1::2]))
    return pairs, results[-1]


def hidden_and_back(order, tiles, parts, weights, out_type, addend=None, cuts=1, twice=True):
    first, count = tiles
    copies, hqr_cuts = (2, 1) if twice else (1, 2)
    sizes = [kept.shape[1] for kept, _ in parts]
    rows = sum(sizes)
    depth = weights[0].shape[1]
    inputs = []
    for pair, size in zip(parts, sizes):
        spec = pl.BlockSpec((3, size, TILE), lambda j: (0, 0, j))
        inputs += [(array, spec) for array in pair]
    n = len(inputs)
    size = rows // hqr_cuts
    inputs += weight_specs(weights, (G, U, PRE), first)
    if addend is not None:
        inputs.append((addend, pl.BlockSpec(addend.shape, lambda j: (0, 0, 0))))

    def body(ins, outs, scratch):
        wg_ref, wu_ref, wd_ref = ins[n : n + 3]
        acc_ref = scratch[0]
        j = pl.program_id(0)
        terms = [ins[m][...] + ins[m + 1][...].astype(jnp.float32) for m in range(0, n, 2)]
        g, u, p = terms[0] if len(terms) == 1 else jnp.concatenate(terms, 1)
        s = jax.nn.sigmoid(g)
        a = g * s
        h = (a * u).astype(jnp.bfloat16)
        q = (p * u * s * (1.0 + g * (1.0 - s))).astype(jnp.bfloat16)
        r = (p * a).astype(jnp.bfloat16)
        for i, value in enumerate((h, q, r)):
            for cut, copy in itertools.product(range(hqr_cuts), range(copies)):
                outs[cut][copy, i] = value[cut * size : (cut + 1) * size]
        out_term = jnp.dot(h, wd_ref[0], preferred_element_type=jnp.float32)
        in_term = contract_cols(q, wg_ref[0]) + contract_cols(r, wu_ref[0])

        @pl.when(j == 0)
        def _():
            acc_ref[0] = out_term
            acc_ref[1] = in_term

        @pl.when(j > 0)
        def _():
            acc_ref[0] += out_term
            acc_ref[1] += in_term

        @pl.when(j == count - 1)
        def _():
            total = acc_ref[...]
            if addend is not None:
                total = total + ins[n + 3][...].astype(jnp.float32)
            step = rows // cuts
            for cut, ref in enumerate(outs[hqr_cuts:]):
                ref[...] = total[:, cut * step : (cut + 1) * step].astype(out_type)

    outputs = [
        (
            jax.ShapeDtypeStruct((copies, 3, size, count * TILE), jnp.bfloat16),
            pl.BlockSpec((copies, 3, size, TILE), lambda j: (0, 0, 0, j)),
        )
    ] * hqr_cuts
    shape = (2, rows // cuts, depth)
    sums_spec = pl.BlockSpec(shape, lambda j: (0, 0, 0))
    outputs += [(jax.ShapeDtypeStruct(shape, out_type), sums_spec)] * cuts
    scratch = [pltpu.VMEM((2, rows, depth), jnp.float32)]
    return order.call(body, "hidden_and_back", 3 + 2.2 * count, count, inputs, outputs, scratch)


def assemble(order, blocks):
    n = len(blocks)
    rows, depth = blocks[0].shape[2:]
    total = 2 * rows * n
    inputs = []
    for block in blocks:
        for part in range(2):
            index = functools.partial(lambda j, part: (0, part, 0, j), part=part)
            inputs.append((block, pl.BlockSpec((2, 1, rows, TILE), index)))

    def body(ins, outs, scratch):
        xt_ref, e_ref = outs
        x_all = scratch[0]
        for b in range(n):
            for d in range(2):
                at = pl.ds((2 * b + d) * rows, rows)
                x_all[at, :] = ins[2 * b][d, 0]
                e_ref[at, :] = ins[2 * b + 1][d, 0]
        xt_ref[...] = x_all[...].T

    outputs = [
        (
            jax.ShapeDtypeStruct((depth, total), jnp.bfloat16),
            pl.BlockSpec((TILE, total), lambda j: (j, 0)),
        ),
        (
            jax.ShapeDtypeStruct((total, depth), jnp.bfloat16),
            pl.BlockSpec((total, TILE), lambda j: (0, j)),
        ),
    ]
    scratch = [pltpu.VMEM((total, TILE), jnp.bfloat16)]
    return order.call(body, "assemble", 5 * n, depth // TILE, inputs, outputs, scratch)


def weight_grads(order, side, tiles, tokens, pieces, width, so_far=None, into=None):
    first, count = tiles
    xt, e_all = tokens
    depth, total = xt.shape
    whole = [
        pl.BlockSpec((depth, total), lambda j: (0, 0), pipeline_mode=pl.Buffered(1)),
        pl.BlockSpec((total, depth), lambda j: (0, 0), pipeline_mode=pl.Buffered(1)),
    ]
    inputs = [(side, pl.BlockSpec(memory_space=pltpu.SMEM)), (xt, whole[0]), (e_all, whole[1])]
    bounds = []
    for _, _, *arrays in pieces:
        at = 0
        for hqr in arrays:
            at = 0 if hqr.shape[0] == 1 else at
            size = hqr.shape[3] // TILE

            def index(j, at, size):
                return 0, 0, 0, jnp.clip(first + j - at, 0, size - 1)

            spec = pl.BlockSpec(
                (hqr.shape[0], 3, hqr.shape[2], TILE),
                functools.partial(index, at=at, size=size),
            )
            inputs.append((hqr, spec))
            bounds.append((at, at + size))
            at += size
    wide = pl.BlockSpec((1, depth, TILE), lambda j: (0, 0, first + j))
    tall = pl.BlockSpec((1, TILE, depth), lambda j: (0, first + j, 0))
    specs = (wide, wide, tall)
    n = len(inputs)
    if so_far is not None:
        inputs += list(zip(so_far, specs))
    aliases = {}
    if into is not None:
        for i, array in enumerate(into):
            aliases[len(inputs)] = i
            inputs.append((array, pl.BlockSpec(memory_space=pl.ANY)))

    def body(ins, outs, scratch):
        hqr_all = scratch[0]
        tile = first + pl.program_id(0)
        m = 0
        for lower, higher, *arrays in pieces:
            for n_array, hqr in enumerate(arrays):

                def take(m=m, starts=(lower, higher), rows=hqr.shape[2]):
                    for d, start in enumerate(starts):
                        for i in range(3):
                            hqr_all[i, pl.ds(start, rows), :] = ins[3 + m][d, i]

                if hqr.shape[0] == 1:
                    upper = ins[0][0] if n_array == 0 else 1 - ins[0][0]
                    start = pl.multiple_of(lower + upper * (higher - lower), 16)
                    take(starts=(start,))
                elif len(arrays) == 1:
                    take()
                else:
                    low, high = bounds[m]
                    pl.when((tile >= low) & (tile < high))(take)
                m += 1
        terms = (
            lambda: jnp.dot(ins[1][...], hqr_all[1], preferred_element_type=jnp.float32),
            lambda: jnp.dot(ins[1][...], hqr_all[2], preferred_element_type=jnp.float32),
            lambda: contract_rows(hqr_all[0], ins[2][...]),
        )
        for i, term in enumerate(terms):
            value = term()
            if so_far is not None:
                value = value + ins[n + i][0].astype(jnp.float32)
            outs[i][0] = value.astype(jnp.bfloat16)

    shapes = ((1, depth, width), (1, depth, width), (1, width, depth))
    outputs = [
        (jax.ShapeDtypeStruct(shape, jnp.bfloat16), spec) for shape, spec in zip(shapes, specs)
    ]
    scratch = [pltpu.VMEM((3, total, TILE), jnp.bfloat16)]
    return order.call(
        body, "weight_grads", 4 + 4 * count, count, inputs, outputs, scratch, aliases=aliases.items()
    )


def add_row_sums(order, own_sums, near_sums, far_sums, acts, cotangent):
    rows, depth = acts.shape[2:]
    cuts = len(far_sums)
    step = rows // cuts
    spec = pl.BlockSpec((2, step, depth), lambda j: (0, j, 0))
    each = pl.BlockSpec((2, step, depth), lambda j: (0, 0, 0))
    token_spec = pl.BlockSpec((1, 1, step, depth), lambda j: (0, 0, j, 0))
    inputs = [(own_sums, spec), (acts, token_spec), (cotangent, token_spec)]
    inputs += [(array, each) for array in (*near_sums, *far_sums)]

    def body(ins, outs, _):
        def add(j):
            for i in range(2):
                total = ins[0][i] + ins[3 + j][i].astype(jnp.float32)
                total += ins[3 + cuts + j][i].astype(jnp.float32)
                total += ins[1 + i][0, 0].astype(jnp.float32)
                outs[i][0, 0] = total.astype(jnp.bfloat16)

        for j in range(cuts):
            pl.when(pl.program_id(0) == j)(functools.partial(add, j))

    outputs = [(jax.ShapeDtypeStruct(acts.shape, jnp.bfloat16), token_spec)] * 2
    return order.call(body, "add_row_sums", 5, cuts, inputs, outputs)


def two_by_four(acts, cotangent, w_gate, w_up, w_down):
    near, far, across = 0, 1, 2
    rows = acts.shape[2]
    half = rows // 2
    width = w_gate.shape[2]
    n_tiles = width // TILE
    weights = (w_gate, w_up, w_down)
    side = lax.axis_index("dp").astype(jnp.int32).reshape(1)
    order = Order()

    sources = {"own": (acts, cotangent)}

    def gather(block, origin, bit):
        sources[block] = tuple(from_partner(array, "grid", bit) for array in sources[origin])

    gather("near", "own", near)
    gather("far", "own", far)

    a = max(1, n_tiles * 3 // 7)
    every = (0, n_tiles)
    chunks = {"c0": (0, a), "c1": (a, n_tiles - a)}
    own, ready, got, pairs = {}, {}, {}, {}

    def compute(names, units, tiles, block, pack=False):
        results, pair = partials(order, units, tiles, sources[block], weights, pack=pack)
        for name, (kept, rounded) in zip(names, results):
            own[name], ready[name] = kept, rounded
        if pack:
            pairs[block] = order.need(both_replicas(pair), 0)

    def send(name, after=()):
        rounded = ready[name]
        if after:
            rounded = order.hold(rounded, [got[key] for key in after])
        got[name] = from_partner(rounded, "grid", across)

    hqr, sums = {}, {}

    def both_replicas(pair):
        return lax.all_to_all(pair, "dp", 0, 0, tiled=True)

    def finish(name, tiles, parts=None, addend=None, calls=99):
        parts = [(own[key], got[key]) for key in parts or [name]]
        cuts = parts[0][0].shape[1] * len(parts) // half if tiles == every else 1
        out_type = jnp.bfloat16 if tiles == every else jnp.float32
        twice = name not in ("fa", "fb")
        found, *rest = hidden_and_back(
            order, tiles, parts, weights, out_type, addend, cuts, twice
        )
        if twice:
            hqr[name] = (order.need(both_replicas(found), calls),)
        else:
            for cut, part in enumerate((found, rest.pop(0))):
                hqr[name, cut] = (part, order.need(from_partner(part, "dp", 0), calls))
        sums[name] = rest

    def pieces_of(*groups):
        found = []
        at = 0
        for group in groups:
            size = sum(hqr[names[0]][0].shape[2] for names in group)
            for names in group:
                found.append((at, at + size, *(array for name in names for array in hqr[name])))
                at += hqr[names[0]][0].shape[2]
            at += size
        return found

    def pass_on(array, bit, calls):
        return order.need(from_partner(array, "grid", bit), calls)

    def collect(*names):
        return assemble(order, [pairs[name] for name in names])

    gup = (G, U, PRE)
    everything = [(gup, 0, rows)]
    halves = [(gup, 0, half), (gup, half, half)]
    compute(["c0"], everything, chunks["c0"], "own")
    send("c0")
    compute(["c1"], everything, chunks["c1"], "own", pack=True)
    compute(["near"], everything, every, "near", pack=True)
    send("near")
    finish("c0", chunks["c0"], calls=1)
    sources["far"] = tuple(order.hold(array, []) for array in sources["far"])
    gather("both", "far", near)
    compute(["fa", "fb"], halves, every, "far", pack=True)
    send("c1", ["c0"])
    early = collect("near", "own")
    compute(["ba", "bb"], halves, every, "both", pack=True)
    send("ba")
    late = collect("both", "far")
    send("bb", ["near"])
    finish("near", every)
    near_sums = [pass_on(array, near, 4) for array in sums["near"]]
    finish("c1", chunks["c1"], addend=sums["c0"][0])
    send("fa", ["ba"])
    early_pieces = pieces_of([["near"]], [["c0", "c1"]])
    mid = n_tiles // 2
    first = weight_grads(order, side, (0, mid), early, early_pieces, width)
    send("fb", ["bb"])
    finish("both", every, parts=["ba", "bb"], calls=1)
    both_sums = [pass_on(sums["both"][0], near, 99)]
    rest = (mid, n_tiles - mid)
    first = weight_grads(order, side, rest, early, early_pieces, width, into=first)
    both_sums.append(pass_on(order.hold(sums["both"][1], []), near, 99))
    far_sums = []
    for name, addend in zip(("fa", "fb"), both_sums):
        finish(name, every, addend=addend, calls=0)
        far_sums.append(pass_on(sums[name][0], far, 99))
    far_names = [[(name, cut)] for name in ("fa", "fb") for cut in range(2)]
    late_pieces = pieces_of([["both"]], far_names)
    grads = weight_grads(order, side, every, late, late_pieces, width, first)
    outs = add_row_sums(order, sums["c1"][0], near_sums, far_sums, acts, cotangent)
    return (*outs, *grads)


def per_device(acts, cotangent, w_gate, w_up, w_down):
    fits = acts.shape[2] % 64 == 0 and acts.shape[3] % TILE == 0 and w_gate.shape[2] % TILE == 0
    if lax.axis_size("grid") == 8 and lax.axis_size("dp") == 2 and fits:
        return two_by_four(acts, cotangent, w_gate, w_up, w_down)
    return any_grid(acts, cotangent, w_gate, w_up, w_down)


def solution(mesh):
    return jax.shard_map(
        per_device,
        mesh=mesh,
        in_specs=(
            P(("groups", "dp"), "grid", None, None),
            P(("groups", "dp"), "grid", None, None),
            P("grid", None, None),
            P("grid", None, None),
            P("grid", None, None),
        ),
        out_specs=(
            P(("groups", "dp"), "grid", None, None),
            P(("groups", "dp"), "grid", None, None),
            P(("groups", "grid"), None, None),
            P(("groups", "grid"), None, None),
            P(("groups", "grid"), None, None),
        ),
        check_vma=False,
    )
```

```python
import functools
import itertools

import jax
import jax.numpy as jnp
from jax import lax
from jax.experimental import pallas as pl
from jax.experimental.pallas import tpu as pltpu
from jax.sharding import PartitionSpec as P

VMEM_BYTES = 62 * 1024 * 1024
TILE = 256
COST_SCALE = 0.08e9
G, U, PRE = 0, 1, 2


def from_partner(block, axis, stride):
    count = lax.axis_size(axis)
    route = []
    for low in range(count):
        high = low | 1 << stride
        if high != low and high < count:
            route += [(low, high), (high, low)]
    return lax.ppermute(block, axis, route)


def contract_rows(left, right):
    return lax.dot_general(
        left, right, (((0,), (0,)), ((), ())), preferred_element_type=jnp.float32
    )


def contract_cols(left, right):
    return lax.dot_general(
        left, right, (((1,), (1,)), ((), ())), preferred_element_type=jnp.float32
    )


def order_pair(is_upper, mine, other, dim=1):
    return jnp.where(
        is_upper, jnp.concatenate([other, mine], dim), jnp.concatenate([mine, other], dim)
    )


def column_sum(partial_term, total_rows, col_bits, row_bits, my_row):
    result_sum = partial_term(0, total_rows)
    for level_bit in range(row_bits - 1, -1, -1):
        half_rows = result_sum.shape[1] // 2
        lower_half = result_sum[:, :half_rows]
        upper_half = result_sum[:, half_rows:]
        is_upper = my_row >> level_bit & 1 == 1
        kept_half = jnp.where(is_upper, upper_half, lower_half)
        given_half = jnp.where(is_upper, lower_half, upper_half)
        result_sum = kept_half + from_partner(
            given_half.astype(jnp.bfloat16), "grid", col_bits + level_bit
        ).astype(given_half.dtype)
    return result_sum


def column_gather(pieces, col_bits, row_bits, my_row):
    for level_bit in range(row_bits):
        partner = from_partner(pieces, "grid", col_bits + level_bit)
        pieces = order_pair(my_row >> level_bit & 1 == 1, pieces, partner)
    return pieces


def row_sum(full_sum, col_bits, my_col):
    for level_bit in range(col_bits - 1, -1, -1):
        half_rows = full_sum.shape[0] // 2
        lower_half = full_sum[:half_rows]
        upper_half = full_sum[half_rows:]
        is_upper = my_col >> level_bit & 1 == 1
        kept_half = jnp.where(is_upper, upper_half, lower_half)
        given_half = jnp.where(is_upper, lower_half, upper_half)
        full_sum = kept_half + from_partner(
            given_half.astype(jnp.bfloat16), "grid", level_bit
        ).astype(given_half.dtype)
    return full_sum


def any_grid(acts, cotangent, w_gate, w_up, w_down):
    grid_size = lax.axis_size("grid")
    grid_cols = min(8, grid_size // 2)
    grid_rows = grid_size // grid_cols
    col_bits = grid_cols.bit_length() - 1
    row_bits = grid_rows.bit_length() - 1
    position = lax.axis_index("grid")
    my_row = position // grid_cols
    my_col = position % grid_cols
    own_acts = acts[0, 0]
    own_grads = cotangent[0, 0]
    gate_tile = w_gate[0]
    up_tile = w_up[0]
    down_tile = w_down[0]
    gathered = jnp.stack([own_acts, own_grads])
    for level_bit in range(col_bits):
        partner = from_partner(gathered, "grid", level_bit)
        gathered = order_pair(my_col >> level_bit & 1 == 1, gathered, partner)
    inputs_row = gathered[0]
    out_grad_row = gathered[1]
    total_rows = inputs_row.shape[0]

    def gate_up_term(row_start, row_count):
        return jnp.stack(
            [
                jnp.dot(inputs_row, gate_tile, preferred_element_type=jnp.float32),
                jnp.dot(inputs_row, up_tile, preferred_element_type=jnp.float32),
            ]
        )

    summed = column_sum(gate_up_term, total_rows, col_bits, row_bits, my_row)
    gate_pre = summed[0]
    up_proj = summed[1]
    sigmoid_g = jax.nn.sigmoid(gate_pre)
    activated = gate_pre * sigmoid_g
    hidden = (activated * up_proj).astype(jnp.bfloat16)
    hidden_full = column_gather(hidden[None], col_bits, row_bits, my_row)[0]
    output_sum = row_sum(
        jnp.dot(hidden_full, down_tile, preferred_element_type=jnp.float32), col_bits, my_col
    )
    block_out = (own_acts.astype(jnp.float32) + output_sum).astype(jnp.bfloat16)

    def hidden_grad_term(row_start, row_count):
        return contract_cols(out_grad_row, down_tile)[None]

    hidden_grad = column_sum(hidden_grad_term, total_rows, col_bits, row_bits, my_row)[0]
    gate_back = (hidden_grad * up_proj * sigmoid_g * (1.0 + gate_pre * (1.0 - sigmoid_g))).astype(
        jnp.bfloat16
    )
    up_back = (hidden_grad * activated).astype(jnp.bfloat16)
    backs_full = column_gather(jnp.stack([gate_back, up_back]), col_bits, row_bits, my_row)
    down_local = contract_rows(hidden_full, out_grad_row)
    input_part = contract_cols(backs_full[0], gate_tile) + contract_cols(backs_full[1], up_tile)
    input_sum = row_sum(input_part, col_bits, my_col)
    input_grad = (own_grads.astype(jnp.float32) + input_sum).astype(jnp.bfloat16)
    gate_local = contract_rows(inputs_row, backs_full[0])
    up_local = contract_rows(inputs_row, backs_full[1])
    gate_total, up_total, down_total = (
        lax.psum(gate_local.astype(jnp.bfloat16), "dp").astype(jnp.float32),
        lax.psum(up_local.astype(jnp.bfloat16), "dp").astype(jnp.float32),
        lax.psum(down_local.astype(jnp.bfloat16), "dp").astype(jnp.float32),
    )
    return (
        block_out[None, None],
        input_grad[None, None],
        gate_total.astype(jnp.bfloat16)[None],
        up_total.astype(jnp.bfloat16)[None],
        down_total.astype(jnp.bfloat16)[None],
    )


class Order:
    def __init__(self):
        self.token = None
        self.calls = 0
        self.due = []

    def need(self, array, calls):
        self.due.append((self.calls + calls, array))
        return array

    def call(self, body, name, cost, steps, inputs, outputs, scratch=(), after=(), aliases=()):
        after = list(after) + ([] if self.token is None else [self.token])
        after += [array for call, array in self.due if call <= self.calls]
        self.due = [(call, array) for call, array in self.due if call > self.calls]
        self.calls += 1
        n_in, n_after, n_out = len(inputs), len(after), len(outputs)

        def kernel(*refs):
            ins = refs[:n_in]
            outs = refs[n_in + n_after : n_in + n_after + n_out]
            refs[n_in + n_after + n_out][...] = jnp.zeros((8, 128), jnp.float32)
            body(ins, outs, refs[n_in + n_after + n_out + 1 :])

        *results, self.token = pl.pallas_call(
            kernel,
            name=name,
            grid=(steps,),
            in_specs=[spec for _, spec in inputs]
            + [pl.BlockSpec(memory_space=pl.ANY) for _ in after],
            out_specs=[spec for _, spec in outputs] + [pl.BlockSpec((8, 128), lambda j: (0, 0))],
            out_shape=[shape for shape, _ in outputs]
            + [jax.ShapeDtypeStruct((8, 128), jnp.float32)],
            scratch_shapes=list(scratch),
            input_output_aliases=dict(aliases),
            cost_estimate=pl.CostEstimate(
                flops=int(cost * COST_SCALE), bytes_accessed=0, transcendentals=0
            ),
            compiler_params=pltpu.CompilerParams(vmem_limit_bytes=VMEM_BYTES),
        )(*[array for array, _ in inputs], *after)
        return results

    def hold(self, array, after):
        inputs = [(array, pl.BlockSpec(memory_space=pl.ANY))]
        outputs = [(jax.ShapeDtypeStruct(array.shape, array.dtype), inputs[0][1])]
        return self.call(
            lambda *_: None, "hold", 0.6, 1, inputs, outputs, after=after, aliases={0: 0}.items()
        )[0]


def weight_specs(weights, kinds, first):
    gate, up, down = weights
    depth = gate.shape[1]
    wide = pl.BlockSpec((1, depth, TILE), lambda j: (0, 0, first + j))
    tall = pl.BlockSpec((1, TILE, depth), lambda j: (0, first + j, 0))
    return [((gate, up, down)[kind], tall if kind == PRE else wide) for kind in kinds]


def partials(order, units, tiles, sources, weights, after=(), pack=False):
    first, count = tiles
    rows, depth = sources[0].shape[2:]
    kinds = [kind for kind in (G, U, PRE) if any(kind in unit[0] for unit in units)]
    token_spec = pl.BlockSpec((1, 1, rows, depth), lambda j: (0, 0, 0, 0))
    inputs = [(sources[kind == PRE], token_spec) for kind in kinds]
    inputs += weight_specs(weights, kinds, first)
    n = len(kinds)

    def body(ins, outs, _):
        for i, kind in enumerate(kinds):
            left, right = ins[i][0, 0], ins[n + i][0]
            if kind == PRE:
                term = contract_cols(left, right)
            else:
                term = jnp.dot(left, right, preferred_element_type=jnp.float32)
            for m, (unit_kinds, start, size) in enumerate(units):
                if kind in unit_kinds:
                    at = unit_kinds.index(kind)
                    outs[2 * m][at] = term[start : start + size]
                    outs[2 * m + 1][at] = term[start : start + size].astype(jnp.bfloat16)
        if pack:

            @pl.when(pl.program_id(0) == 0)
            def _():
                for d in range(2):
                    outs[-1][d, 0] = ins[kinds.index(G)][0, 0]
                    outs[-1][d, 1] = ins[kinds.index(PRE)][0, 0]

    outputs = []
    for unit_kinds, _, size in units:
        shape = (len(unit_kinds), size, count * TILE)
        spec = pl.BlockSpec((len(unit_kinds), size, TILE), lambda j: (0, 0, j))
        outputs.append((jax.ShapeDtypeStruct(shape, jnp.float32), spec))
        outputs.append((jax.ShapeDtypeStruct(shape, jnp.bfloat16), spec))
    if pack:
        shape = (2, 2, rows, depth)
        spec = pl.BlockSpec(shape, lambda j: (0, 0, 0, 0))
        outputs.append((jax.ShapeDtypeStruct(shape, jnp.bfloat16), spec))
    cost = (1 + 0.8 * count) * n
    results = order.call(body, "partials", cost, count, inputs, outputs, after=after)
    pairs = list(zip(results[: 2 * len(units) : 2], results[1::2]))
    return pairs, results[-1]


def hidden_and_back(order, tiles, parts, weights, out_type, addend=(), cuts=None, twice=True):
    first, count = tiles
    copies, hqr_cuts = (2, 1) if twice else (1, 2)
    sizes = [kept.shape[1] for kept, _ in parts]
    rows = sum(sizes)
    depth = weights[0].shape[1]
    inputs = []
    for pair, size in zip(parts, sizes):
        spec = pl.BlockSpec((3, size, TILE), lambda j: (0, 0, j))
        inputs += [(array, spec) for array in pair]
    n = len(inputs)
    size = rows // hqr_cuts
    inputs += weight_specs(weights, (G, U, PRE), first)
    inputs += [(array, pl.BlockSpec(array.shape, lambda j: (0, 0, 0))) for array in addend]
    cuts = cuts or [rows]

    def body(ins, outs, scratch):
        wg_ref, wu_ref, wd_ref = ins[n : n + 3]
        acc_ref = scratch[0]
        j = pl.program_id(0)
        terms = [ins[m][...] + ins[m + 1][...].astype(jnp.float32) for m in range(0, n, 2)]
        g, u, p = terms[0] if len(terms) == 1 else jnp.concatenate(terms, 1)
        s = jax.nn.sigmoid(g)
        a = g * s
        h = (a * u).astype(jnp.bfloat16)
        q = (p * u * s * (1.0 + g * (1.0 - s))).astype(jnp.bfloat16)
        r = (p * a).astype(jnp.bfloat16)
        for i, value in enumerate((h, q, r)):
            for cut, copy in itertools.product(range(hqr_cuts), range(copies)):
                outs[cut][copy, i] = value[cut * size : (cut + 1) * size]
        out_term = jnp.dot(h, wd_ref[0], preferred_element_type=jnp.float32)
        in_term = contract_cols(q, wg_ref[0]) + contract_cols(r, wu_ref[0])

        @pl.when(j == 0)
        def _():
            acc_ref[0] = out_term
            acc_ref[1] = in_term

        @pl.when(j > 0)
        def _():
            acc_ref[0] += out_term
            acc_ref[1] += in_term

        @pl.when(j == count - 1)
        def _():
            at = 0
            for ref in ins[n + 3 :]:
                acc_ref[:, at : at + ref.shape[1]] += ref[...].astype(jnp.float32)
                at += ref.shape[1]
            at = 0
            for ref in outs[hqr_cuts:]:
                ref[...] = acc_ref[:, at : at + ref.shape[1]].astype(out_type)
                at += ref.shape[1]

    outputs = [
        (
            jax.ShapeDtypeStruct((copies, 3, size, count * TILE), jnp.bfloat16),
            pl.BlockSpec((copies, 3, size, TILE), lambda j: (0, 0, 0, j)),
        )
    ] * hqr_cuts
    for cut in cuts:
        shape = (2, cut, depth)
        spec = pl.BlockSpec(shape, lambda j: (0, 0, 0))
        outputs.append((jax.ShapeDtypeStruct(shape, out_type), spec))
    scratch = [pltpu.VMEM((2, rows, depth), jnp.float32)]
    return order.call(body, "hidden_and_back", 3 + 2.2 * count, count, inputs, outputs, scratch)


def assemble(order, blocks):
    n = len(blocks)
    rows, depth = blocks[0].shape[2:]
    total = 2 * rows * n
    inputs = []
    for block in blocks:
        for part in range(2):
            index = functools.partial(lambda j, part: (0, part, 0, j), part=part)
            inputs.append((block, pl.BlockSpec((2, 1, rows, TILE), index)))

    def body(ins, outs, scratch):
        xt_ref, e_ref = outs
        x_all = scratch[0]
        for b in range(n):
            for d in range(2):
                at = pl.ds((2 * b + d) * rows, rows)
                x_all[at, :] = ins[2 * b][d, 0]
                e_ref[at, :] = ins[2 * b + 1][d, 0]
        xt_ref[...] = x_all[...].T

    outputs = [
        (
            jax.ShapeDtypeStruct((depth, total), jnp.bfloat16),
            pl.BlockSpec((TILE, total), lambda j: (j, 0)),
        ),
        (
            jax.ShapeDtypeStruct((total, depth), jnp.bfloat16),
            pl.BlockSpec((total, TILE), lambda j: (0, j)),
        ),
    ]
    scratch = [pltpu.VMEM((total, TILE), jnp.bfloat16)]
    return order.call(body, "assemble", 5 * n, depth // TILE, inputs, outputs, scratch)


def weight_grads(order, side, tiles, tokens, pieces, width, so_far=None, into=None):
    first, count = tiles
    xt, e_all = tokens
    depth, total = xt.shape
    whole = [
        pl.BlockSpec((depth, total), lambda j: (0, 0), pipeline_mode=pl.Buffered(1)),
        pl.BlockSpec((total, depth), lambda j: (0, 0), pipeline_mode=pl.Buffered(1)),
    ]
    inputs = [(side, pl.BlockSpec(memory_space=pltpu.SMEM)), (xt, whole[0]), (e_all, whole[1])]
    bounds = []
    for _, _, *arrays in pieces:
        at = 0
        for hqr in arrays:
            at = 0 if hqr.shape[0] == 1 else at
            size = hqr.shape[3] // TILE

            def index(j, at, size):
                return 0, 0, 0, jnp.clip(first + j - at, 0, size - 1)

            spec = pl.BlockSpec(
                (hqr.shape[0], 3, hqr.shape[2], TILE),
                functools.partial(index, at=at, size=size),
            )
            inputs.append((hqr, spec))
            bounds.append((at, at + size))
            at += size
    wide = pl.BlockSpec((1, depth, TILE), lambda j: (0, 0, first + j))
    tall = pl.BlockSpec((1, TILE, depth), lambda j: (0, first + j, 0))
    specs = (wide, wide, tall)
    n = len(inputs)
    if so_far is not None:
        inputs += list(zip(so_far, specs))
    aliases = {}
    if into is not None:
        for i, array in enumerate(into):
            aliases[len(inputs)] = i
            inputs.append((array, pl.BlockSpec(memory_space=pl.ANY)))

    def body(ins, outs, scratch):
        hqr_all = scratch[0]
        tile = first + pl.program_id(0)
        m = 0
        for lower, higher, *arrays in pieces:
            for n_array, hqr in enumerate(arrays):

                def take(m=m, starts=(lower, higher), rows=hqr.shape[2]):
                    for d, start in enumerate(starts):
                        for i in range(3):
                            hqr_all[i, pl.ds(start, rows), :] = ins[3 + m][d, i]

                if hqr.shape[0] == 1:
                    upper = ins[0][0] if n_array == 0 else 1 - ins[0][0]
                    start = pl.multiple_of(lower + upper * (higher - lower), 16)
                    take(starts=(start,))
                elif len(arrays) == 1:
                    take()
                else:
                    low, high = bounds[m]
                    pl.when((tile >= low) & (tile < high))(take)
                m += 1
        terms = (
            lambda: jnp.dot(ins[1][...], hqr_all[1], preferred_element_type=jnp.float32),
            lambda: jnp.dot(ins[1][...], hqr_all[2], preferred_element_type=jnp.float32),
            lambda: contract_rows(hqr_all[0], ins[2][...]),
        )
        for i, term in enumerate(terms):
            value = term()
            if so_far is not None:
                value = value + ins[n + i][0].astype(jnp.float32)
            outs[i][0] = value.astype(jnp.bfloat16)

    shapes = ((1, depth, width), (1, depth, width), (1, width, depth))
    outputs = [
        (jax.ShapeDtypeStruct(shape, jnp.bfloat16), spec) for shape, spec in zip(shapes, specs)
    ]
    scratch = [pltpu.VMEM((3, total, TILE), jnp.bfloat16)]
    return order.call(
        body, "weight_grads", 4 + 4 * count, count, inputs, outputs, scratch, aliases=aliases.items()
    )


def add_row_sums(order, own_sums, near_sums, far_sums, acts, cotangent):
    rows, depth = acts.shape[2:]
    cuts = len(far_sums)
    step = rows // cuts
    spec = pl.BlockSpec((2, step, depth), lambda j: (0, j, 0))
    each = pl.BlockSpec((2, step, depth), lambda j: (0, 0, 0))
    token_spec = pl.BlockSpec((1, 1, step, depth), lambda j: (0, 0, j, 0))
    inputs = [(own_sums, spec), (acts, token_spec), (cotangent, token_spec)]
    inputs += [(array, each) for array in (*near_sums, *far_sums)]

    def body(ins, outs, _):
        def add(j):
            for i in range(2):
                total = ins[0][i] + ins[3 + j][i].astype(jnp.float32)
                total += ins[3 + cuts + j][i].astype(jnp.float32)
                total += ins[1 + i][0, 0].astype(jnp.float32)
                outs[i][0, 0] = total.astype(jnp.bfloat16)

        for j in range(cuts):
            pl.when(pl.program_id(0) == j)(functools.partial(add, j))

    outputs = [(jax.ShapeDtypeStruct(acts.shape, jnp.bfloat16), token_spec)] * 2
    return order.call(body, "add_row_sums", 5, cuts, inputs, outputs)


def two_by_four(acts, cotangent, w_gate, w_up, w_down):
    near, far, across = 0, 1, 2
    rows = acts.shape[2]
    half = rows // 2
    width = w_gate.shape[2]
    n_tiles = width // TILE
    weights = (w_gate, w_up, w_down)
    side = lax.axis_index("dp").astype(jnp.int32).reshape(1)
    order = Order()

    sources = {"own": (acts, cotangent)}

    def gather(block, origin, bit):
        sources[block] = tuple(from_partner(array, "grid", bit) for array in sources[origin])

    gather("near", "own", near)
    gather("far", "own", far)

    a = max(1, n_tiles * 3 // 7)
    every = (0, n_tiles)
    chunks = {"c0": (0, a), "c1": (a, n_tiles - a)}
    own, ready, got, pairs = {}, {}, {}, {}

    def compute(names, units, tiles, block, pack=False):
        results, pair = partials(order, units, tiles, sources[block], weights, pack=pack)
        for name, (kept, rounded) in zip(names, results):
            own[name], ready[name] = kept, rounded
        if pack:
            pairs[block] = order.need(both_replicas(pair), 0)

    def send(name, after=()):
        rounded = ready[name]
        if after:
            rounded = order.hold(rounded, [got[key] for key in after])
        got[name] = from_partner(rounded, "grid", across)

    hqr, sums = {}, {}

    def both_replicas(pair):
        return lax.all_to_all(pair, "dp", 0, 0, tiled=True)

    def finish(name, tiles, parts=None, addend=(), calls=99, cuts=None):
        parts = [(own[key], got[key]) for key in parts or [name]]
        out_type = jnp.bfloat16 if tiles == every else jnp.float32
        twice = name not in ("fa", "fb")
        found, *rest = hidden_and_back(
            order, tiles, parts, weights, out_type, addend, cuts, twice
        )
        if twice:
            hqr[name] = (order.need(both_replicas(found), calls),)
        else:
            for cut, part in enumerate((found, rest.pop(0))):
                hqr[name, cut] = (part, order.need(from_partner(part, "dp", 0), calls))
        sums[name] = rest

    def pieces_of(*groups):
        found = []
        at = 0
        for group in groups:
            size = sum(hqr[names[0]][0].shape[2] for names in group)
            for names in group:
                found.append((at, at + size, *(array for name in names for array in hqr[name])))
                at += hqr[names[0]][0].shape[2]
            at += size
        return found

    def pass_on(array, bit, calls):
        return order.need(from_partner(array, "grid", bit), calls)

    def collect(*names):
        return assemble(order, [pairs[name] for name in names])

    gup = (G, U, PRE)
    everything = [(gup, 0, rows)]
    halves = [(gup, 0, half), (gup, half, half)]
    compute(["c0"], everything, chunks["c0"], "own")
    send("c0")
    compute(["c1"], everything, chunks["c1"], "own", pack=True)
    compute(["near"], everything, every, "near", pack=True)
    send("near")
    finish("c0", chunks["c0"], calls=1)
    sources["far"] = tuple(order.hold(array, []) for array in sources["far"])
    gather("both", "far", near)
    compute(["fa", "fb"], halves, every, "far", pack=True)
    send("c1", ["c0"])
    early = collect("near", "own")
    compute(["ba", "bb"], halves, every, "both", pack=True)
    send("ba")
    late = collect("both", "far")
    send("bb", ["near"])
    finish("near", every, calls=0, cuts=[half] * 2)
    near_sums = [pass_on(array, near, 3) for array in sums["near"]]
    early_pieces = pieces_of([["near"]], [["c0"]])
    first = weight_grads(order, side, chunks["c0"], early, early_pieces, width)
    finish("c1", chunks["c1"], addend=sums["c0"], calls=0)
    early_pieces = pieces_of([["near"]], [["c0", "c1"]])
    send("fa", ["ba", "bb"])
    finish("both", every, parts=["ba", "bb"], calls=3, cuts=[half // 2] * 2 + [half])
    send("fb", ["bb"])
    *leading, trailing = sums["both"]
    both_sums = [[pass_on(array, near, 99) for array in leading]]
    first = weight_grads(order, side, chunks["c1"], early, early_pieces, width, into=first)
    both_sums.append([pass_on(order.hold(trailing, []), near, 99)])
    far_sums = []
    for name, addend in zip(("fa", "fb"), both_sums):
        finish(name, every, addend=addend, calls=0)
        far_sums.append(pass_on(sums[name][0], far, 99))
    far_names = [[(name, cut)] for name in ("fa", "fb") for cut in range(2)]
    late_pieces = pieces_of([["both"]], far_names)
    grads = weight_grads(order, side, every, late, late_pieces, width, first)
    outs = add_row_sums(order, sums["c1"][0], near_sums, far_sums, acts, cotangent)
    return (*outs, *grads)


def per_device(acts, cotangent, w_gate, w_up, w_down):
    fits = acts.shape[2] % 64 == 0 and acts.shape[3] % TILE == 0 and w_gate.shape[2] % TILE == 0
    if lax.axis_size("grid") == 8 and lax.axis_size("dp") == 2 and fits:
        return two_by_four(acts, cotangent, w_gate, w_up, w_down)
    return any_grid(acts, cotangent, w_gate, w_up, w_down)


def solution(mesh):
    return jax.shard_map(
        per_device,
        mesh=mesh,
        in_specs=(
            P(("groups", "dp"), "grid", None, None),
            P(("groups", "dp"), "grid", None, None),
            P("grid", None, None),
            P("grid", None, None),
            P("grid", None, None),
        ),
        out_specs=(
            P(("groups", "dp"), "grid", None, None),
            P(("groups", "dp"), "grid", None, None),
            P(("groups", "grid"), None, None),
            P(("groups", "grid"), None, None),
            P(("groups", "grid"), None, None),
        ),
        check_vma=False,
    )
```

```python
import functools
import itertools

import jax
import jax.numpy as jnp
from jax import lax
from jax.experimental import pallas as pl
from jax.experimental.pallas import tpu as pltpu
from jax.sharding import PartitionSpec as P

VMEM_BYTES = 62 * 1024 * 1024
TILE = 256
COST_SCALE = 0.2e9
G, U, PRE = 0, 1, 2


def from_partner(block, axis, stride):
    count = lax.axis_size(axis)
    route = []
    for low in range(count):
        high = low | 1 << stride
        if high != low and high < count:
            route += [(low, high), (high, low)]
    return lax.ppermute(block, axis, route)


def contract_rows(left, right):
    return lax.dot_general(
        left, right, (((0,), (0,)), ((), ())), preferred_element_type=jnp.float32
    )


def contract_cols(left, right):
    return lax.dot_general(
        left, right, (((1,), (1,)), ((), ())), preferred_element_type=jnp.float32
    )


def order_pair(is_upper, mine, other, dim=1):
    return jnp.where(
        is_upper, jnp.concatenate([other, mine], dim), jnp.concatenate([mine, other], dim)
    )


def column_sum(partial_term, total_rows, col_bits, row_bits, my_row):
    result_sum = partial_term(0, total_rows)
    for level_bit in range(row_bits - 1, -1, -1):
        half_rows = result_sum.shape[1] // 2
        lower_half = result_sum[:, :half_rows]
        upper_half = result_sum[:, half_rows:]
        is_upper = my_row >> level_bit & 1 == 1
        kept_half = jnp.where(is_upper, upper_half, lower_half)
        given_half = jnp.where(is_upper, lower_half, upper_half)
        result_sum = kept_half + from_partner(
            given_half.astype(jnp.bfloat16), "grid", col_bits + level_bit
        ).astype(given_half.dtype)
    return result_sum


def column_gather(pieces, col_bits, row_bits, my_row):
    for level_bit in range(row_bits):
        partner = from_partner(pieces, "grid", col_bits + level_bit)
        pieces = order_pair(my_row >> level_bit & 1 == 1, pieces, partner)
    return pieces


def row_sum(full_sum, col_bits, my_col):
    for level_bit in range(col_bits - 1, -1, -1):
        half_rows = full_sum.shape[0] // 2
        lower_half = full_sum[:half_rows]
        upper_half = full_sum[half_rows:]
        is_upper = my_col >> level_bit & 1 == 1
        kept_half = jnp.where(is_upper, upper_half, lower_half)
        given_half = jnp.where(is_upper, lower_half, upper_half)
        full_sum = kept_half + from_partner(
            given_half.astype(jnp.bfloat16), "grid", level_bit
        ).astype(given_half.dtype)
    return full_sum


def any_grid(acts, cotangent, w_gate, w_up, w_down):
    grid_size = lax.axis_size("grid")
    grid_cols = min(8, grid_size // 2)
    grid_rows = grid_size // grid_cols
    col_bits = grid_cols.bit_length() - 1
    row_bits = grid_rows.bit_length() - 1
    position = lax.axis_index("grid")
    my_row = position // grid_cols
    my_col = position % grid_cols
    own_acts = acts[0, 0]
    own_grads = cotangent[0, 0]
    gate_tile = w_gate[0]
    up_tile = w_up[0]
    down_tile = w_down[0]
    gathered = jnp.stack([own_acts, own_grads])
    for level_bit in range(col_bits):
        partner = from_partner(gathered, "grid", level_bit)
        gathered = order_pair(my_col >> level_bit & 1 == 1, gathered, partner)
    inputs_row = gathered[0]
    out_grad_row = gathered[1]
    total_rows = inputs_row.shape[0]

    def gate_up_term(row_start, row_count):
        return jnp.stack(
            [
                jnp.dot(inputs_row, gate_tile, preferred_element_type=jnp.float32),
                jnp.dot(inputs_row, up_tile, preferred_element_type=jnp.float32),
            ]
        )

    summed = column_sum(gate_up_term, total_rows, col_bits, row_bits, my_row)
    gate_pre = summed[0]
    up_proj = summed[1]
    sigmoid_g = jax.nn.sigmoid(gate_pre)
    activated = gate_pre * sigmoid_g
    hidden = (activated * up_proj).astype(jnp.bfloat16)
    hidden_full = column_gather(hidden[None], col_bits, row_bits, my_row)[0]
    output_sum = row_sum(
        jnp.dot(hidden_full, down_tile, preferred_element_type=jnp.float32), col_bits, my_col
    )
    block_out = (own_acts.astype(jnp.float32) + output_sum).astype(jnp.bfloat16)

    def hidden_grad_term(row_start, row_count):
        return contract_cols(out_grad_row, down_tile)[None]

    hidden_grad = column_sum(hidden_grad_term, total_rows, col_bits, row_bits, my_row)[0]
    gate_back = (hidden_grad * up_proj * sigmoid_g * (1.0 + gate_pre * (1.0 - sigmoid_g))).astype(
        jnp.bfloat16
    )
    up_back = (hidden_grad * activated).astype(jnp.bfloat16)
    backs_full = column_gather(jnp.stack([gate_back, up_back]), col_bits, row_bits, my_row)
    down_local = contract_rows(hidden_full, out_grad_row)
    input_part = contract_cols(backs_full[0], gate_tile) + contract_cols(backs_full[1], up_tile)
    input_sum = row_sum(input_part, col_bits, my_col)
    input_grad = (own_grads.astype(jnp.float32) + input_sum).astype(jnp.bfloat16)
    gate_local = contract_rows(inputs_row, backs_full[0])
    up_local = contract_rows(inputs_row, backs_full[1])
    gate_total, up_total, down_total = (
        lax.psum(gate_local.astype(jnp.bfloat16), "dp").astype(jnp.float32),
        lax.psum(up_local.astype(jnp.bfloat16), "dp").astype(jnp.float32),
        lax.psum(down_local.astype(jnp.bfloat16), "dp").astype(jnp.float32),
    )
    return (
        block_out[None, None],
        input_grad[None, None],
        gate_total.astype(jnp.bfloat16)[None],
        up_total.astype(jnp.bfloat16)[None],
        down_total.astype(jnp.bfloat16)[None],
    )


class Order:
    def __init__(self):
        self.token = None
        self.calls = 0
        self.due = []

    def need(self, array, calls):
        self.due.append((self.calls + calls, array))
        return array

    def call(self, body, name, cost, steps, inputs, outputs, scratch=(), after=(), aliases=()):
        after = list(after) + ([] if self.token is None else [self.token])
        after += [array for call, array in self.due if call <= self.calls]
        self.due = [(call, array) for call, array in self.due if call > self.calls]
        self.calls += 1
        n_in, n_after, n_out = len(inputs), len(after), len(outputs)

        def kernel(*refs):
            ins = refs[:n_in]
            outs = refs[n_in + n_after : n_in + n_after + n_out]
            refs[n_in + n_after + n_out][...] = jnp.zeros((8, 128), jnp.float32)
            body(ins, outs, refs[n_in + n_after + n_out + 1 :])

        *results, self.token = pl.pallas_call(
            kernel,
            name=name,
            grid=(steps,),
            in_specs=[spec for _, spec in inputs]
            + [pl.BlockSpec(memory_space=pl.ANY) for _ in after],
            out_specs=[spec for _, spec in outputs] + [pl.BlockSpec((8, 128), lambda j: (0, 0))],
            out_shape=[shape for shape, _ in outputs]
            + [jax.ShapeDtypeStruct((8, 128), jnp.float32)],
            scratch_shapes=list(scratch),
            input_output_aliases=dict(aliases),
            cost_estimate=pl.CostEstimate(
                flops=int(cost * COST_SCALE), bytes_accessed=0, transcendentals=0
            ),
            compiler_params=pltpu.CompilerParams(vmem_limit_bytes=VMEM_BYTES),
        )(*[array for array, _ in inputs], *after)
        return results

    def hold(self, array, after):
        inputs = [(array, pl.BlockSpec(memory_space=pl.ANY))]
        outputs = [(jax.ShapeDtypeStruct(array.shape, array.dtype), inputs[0][1])]
        return self.call(
            lambda *_: None, "hold", 0.6, 1, inputs, outputs, after=after, aliases={0: 0}.items()
        )[0]


def weight_specs(weights, kinds, first):
    gate, up, down = weights
    depth = gate.shape[1]
    wide = pl.BlockSpec((1, depth, TILE), lambda j: (0, 0, first + j))
    tall = pl.BlockSpec((1, TILE, depth), lambda j: (0, first + j, 0))
    return [((gate, up, down)[kind], tall if kind == PRE else wide) for kind in kinds]


def partials(order, units, tiles, sources, weights, after=(), pack=False):
    first, count = tiles
    rows, depth = sources[0].shape[2:]
    kinds = [kind for kind in (G, U, PRE) if any(kind in unit[0] for unit in units)]
    token_spec = pl.BlockSpec((1, 1, rows, depth), lambda j: (0, 0, 0, 0))
    inputs = [(sources[kind == PRE], token_spec) for kind in kinds]
    inputs += weight_specs(weights, kinds, first)
    n = len(kinds)

    def body(ins, outs, _):
        for i, kind in enumerate(kinds):
            left, right = ins[i][0, 0], ins[n + i][0]
            if kind == PRE:
                term = contract_cols(left, right)
            else:
                term = jnp.dot(left, right, preferred_element_type=jnp.float32)
            for m, (unit_kinds, start, size) in enumerate(units):
                if kind in unit_kinds:
                    at = unit_kinds.index(kind)
                    outs[2 * m][at] = term[start : start + size]
                    outs[2 * m + 1][at] = term[start : start + size].astype(jnp.bfloat16)
        if pack:

            @pl.when(pl.program_id(0) == 0)
            def _():
                for d in range(2):
                    outs[-1][d, 0] = ins[kinds.index(G)][0, 0]
                    outs[-1][d, 1] = ins[kinds.index(PRE)][0, 0]

    outputs = []
    for unit_kinds, _, size in units:
        shape = (len(unit_kinds), size, count * TILE)
        spec = pl.BlockSpec((len(unit_kinds), size, TILE), lambda j: (0, 0, j))
        outputs.append((jax.ShapeDtypeStruct(shape, jnp.float32), spec))
        outputs.append((jax.ShapeDtypeStruct(shape, jnp.bfloat16), spec))
    if pack:
        shape = (2, 2, rows, depth)
        spec = pl.BlockSpec(shape, lambda j: (0, 0, 0, 0))
        outputs.append((jax.ShapeDtypeStruct(shape, jnp.bfloat16), spec))
    cost = (1 + 0.8 * count) * n
    results = order.call(body, "partials", cost, count, inputs, outputs, after=after)
    pairs = list(zip(results[: 2 * len(units) : 2], results[1::2]))
    return pairs, results[-1]


def hidden_and_back(order, tiles, parts, weights, out_type, addend=(), cuts=None, twice=True):
    first, count = tiles
    copies, hqr_cuts = (2, 1) if twice else (1, 2)
    sizes = [kept.shape[1] for kept, _ in parts]
    rows = sum(sizes)
    depth = weights[0].shape[1]
    inputs = []
    for pair, size in zip(parts, sizes):
        spec = pl.BlockSpec((3, size, TILE), lambda j: (0, 0, j))
        inputs += [(array, spec) for array in pair]
    n = len(inputs)
    size = rows // hqr_cuts
    inputs += weight_specs(weights, (G, U, PRE), first)
    inputs += [(array, pl.BlockSpec(array.shape, lambda j: (0, 0, 0))) for array in addend]
    cuts = cuts or [rows]

    def body(ins, outs, scratch):
        wg_ref, wu_ref, wd_ref = ins[n : n + 3]
        acc_ref = scratch[0]
        j = pl.program_id(0)
        terms = [ins[m][...] + ins[m + 1][...].astype(jnp.float32) for m in range(0, n, 2)]
        g, u, p = terms[0] if len(terms) == 1 else jnp.concatenate(terms, 1)
        s = jax.nn.sigmoid(g)
        a = g * s
        h = (a * u).astype(jnp.bfloat16)
        q = (p * u * s * (1.0 + g * (1.0 - s))).astype(jnp.bfloat16)
        r = (p * a).astype(jnp.bfloat16)
        for i, value in enumerate((h, q, r)):
            for cut, copy in itertools.product(range(hqr_cuts), range(copies)):
                outs[cut][copy, i] = value[cut * size : (cut + 1) * size]
        out_term = jnp.dot(h, wd_ref[0], preferred_element_type=jnp.float32)
        in_term = contract_cols(q, wg_ref[0]) + contract_cols(r, wu_ref[0])

        @pl.when(j == 0)
        def _():
            acc_ref[0] = out_term
            acc_ref[1] = in_term

        @pl.when(j > 0)
        def _():
            acc_ref[0] += out_term
            acc_ref[1] += in_term

        @pl.when(j == count - 1)
        def _():
            at = 0
            for ref in ins[n + 3 :]:
                acc_ref[:, at : at + ref.shape[1]] += ref[...].astype(jnp.float32)
                at += ref.shape[1]
            at = 0
            for ref in outs[hqr_cuts:]:
                ref[...] = acc_ref[:, at : at + ref.shape[1]].astype(out_type)
                at += ref.shape[1]

    outputs = [
        (
            jax.ShapeDtypeStruct((copies, 3, size, count * TILE), jnp.bfloat16),
            pl.BlockSpec((copies, 3, size, TILE), lambda j: (0, 0, 0, j)),
        )
    ] * hqr_cuts
    for cut in cuts:
        shape = (2, cut, depth)
        spec = pl.BlockSpec(shape, lambda j: (0, 0, 0))
        outputs.append((jax.ShapeDtypeStruct(shape, out_type), spec))
    scratch = [pltpu.VMEM((2, rows, depth), jnp.float32)]
    return order.call(body, "hidden_and_back", 3 + 2.2 * count, count, inputs, outputs, scratch)


def assemble(order, blocks):
    n = len(blocks)
    rows, depth = blocks[0].shape[2:]
    total = 2 * rows * n
    inputs = []
    for block in blocks:
        for part in range(2):
            index = functools.partial(lambda j, part: (0, part, 0, j), part=part)
            inputs.append((block, pl.BlockSpec((2, 1, rows, TILE), index)))

    def body(ins, outs, scratch):
        xt_ref, e_ref = outs
        x_all = scratch[0]
        for b in range(n):
            for d in range(2):
                at = pl.ds((2 * b + d) * rows, rows)
                x_all[at, :] = ins[2 * b][d, 0]
                e_ref[at, :] = ins[2 * b + 1][d, 0]
        xt_ref[...] = x_all[...].T

    outputs = [
        (
            jax.ShapeDtypeStruct((depth, total), jnp.bfloat16),
            pl.BlockSpec((TILE, total), lambda j: (j, 0)),
        ),
        (
            jax.ShapeDtypeStruct((total, depth), jnp.bfloat16),
            pl.BlockSpec((total, TILE), lambda j: (0, j)),
        ),
    ]
    scratch = [pltpu.VMEM((total, TILE), jnp.bfloat16)]
    return order.call(body, "assemble", 5 * n, depth // TILE, inputs, outputs, scratch)


def weight_grads(order, side, tiles, tokens, pieces, width, so_far=None, into=None):
    first, count = tiles
    xt, e_all = tokens
    depth, total = xt.shape
    whole = [
        pl.BlockSpec((depth, total), lambda j: (0, 0), pipeline_mode=pl.Buffered(1)),
        pl.BlockSpec((total, depth), lambda j: (0, 0), pipeline_mode=pl.Buffered(1)),
    ]
    inputs = [(side, pl.BlockSpec(memory_space=pltpu.SMEM)), (xt, whole[0]), (e_all, whole[1])]
    bounds = []
    for _, _, *arrays in pieces:
        at = 0
        for hqr in arrays:
            at = 0 if hqr.shape[0] == 1 else at
            size = hqr.shape[3] // TILE

            def index(j, at, size):
                return 0, 0, 0, jnp.clip(first + j - at, 0, size - 1)

            spec = pl.BlockSpec(
                (hqr.shape[0], 3, hqr.shape[2], TILE),
                functools.partial(index, at=at, size=size),
            )
            inputs.append((hqr, spec))
            bounds.append((at, at + size))
            at += size
    wide = pl.BlockSpec((1, depth, TILE), lambda j: (0, 0, first + j))
    tall = pl.BlockSpec((1, TILE, depth), lambda j: (0, first + j, 0))
    specs = (wide, wide, tall)
    n = len(inputs)
    if so_far is not None:
        inputs += list(zip(so_far, specs))
    aliases = {}
    if into is not None:
        for i, array in enumerate(into):
            aliases[len(inputs)] = i
            inputs.append((array, pl.BlockSpec(memory_space=pl.ANY)))

    def body(ins, outs, scratch):
        hqr_all = scratch[0]
        tile = first + pl.program_id(0)
        m = 0
        for lower, higher, *arrays in pieces:
            for n_array, hqr in enumerate(arrays):

                def take(m=m, starts=(lower, higher), rows=hqr.shape[2]):
                    for d, start in enumerate(starts):
                        for i in range(3):
                            hqr_all[i, pl.ds(start, rows), :] = ins[3 + m][d, i]

                if hqr.shape[0] == 1:
                    upper = ins[0][0] if n_array == 0 else 1 - ins[0][0]
                    start = pl.multiple_of(lower + upper * (higher - lower), 16)
                    take(starts=(start,))
                elif len(arrays) == 1:
                    take()
                else:
                    low, high = bounds[m]
                    pl.when((tile >= low) & (tile < high))(take)
                m += 1
        terms = (
            lambda: jnp.dot(ins[1][...], hqr_all[1], preferred_element_type=jnp.float32),
            lambda: jnp.dot(ins[1][...], hqr_all[2], preferred_element_type=jnp.float32),
            lambda: contract_rows(hqr_all[0], ins[2][...]),
        )
        for i, term in enumerate(terms):
            value = term()
            if so_far is not None:
                value = value + ins[n + i][0].astype(jnp.float32)
            outs[i][0] = value.astype(jnp.bfloat16)

    shapes = ((1, depth, width), (1, depth, width), (1, width, depth))
    outputs = [
        (jax.ShapeDtypeStruct(shape, jnp.bfloat16), spec) for shape, spec in zip(shapes, specs)
    ]
    scratch = [pltpu.VMEM((3, total, TILE), jnp.bfloat16)]
    return order.call(
        body, "weight_grads", 4 + 2 * count, count, inputs, outputs, scratch, aliases=aliases.items()
    )


def add_row_sums(order, own_sums, near_sums, far_sums, acts, cotangent):
    rows, depth = acts.shape[2:]
    cuts = len(far_sums)
    step = rows // cuts
    spec = pl.BlockSpec((2, step, depth), lambda j: (0, j, 0))
    each = pl.BlockSpec((2, step, depth), lambda j: (0, 0, 0))
    token_spec = pl.BlockSpec((1, 1, step, depth), lambda j: (0, 0, j, 0))
    inputs = [(own_sums, spec), (acts, token_spec), (cotangent, token_spec)]
    inputs += [(array, each) for array in (*near_sums, *far_sums)]

    def body(ins, outs, _):
        def add(j):
            for i in range(2):
                total = ins[0][i] + ins[3 + j][i].astype(jnp.float32)
                total += ins[3 + cuts + j][i].astype(jnp.float32)
                total += ins[1 + i][0, 0].astype(jnp.float32)
                outs[i][0, 0] = total.astype(jnp.bfloat16)

        for j in range(cuts):
            pl.when(pl.program_id(0) == j)(functools.partial(add, j))

    outputs = [(jax.ShapeDtypeStruct(acts.shape, jnp.bfloat16), token_spec)] * 2
    return order.call(body, "add_row_sums", 5, cuts, inputs, outputs)


def two_by_four(acts, cotangent, w_gate, w_up, w_down):
    near, far, across = 0, 1, 2
    rows = acts.shape[2]
    half = rows // 2
    width = w_gate.shape[2]
    n_tiles = width // TILE
    weights = (w_gate, w_up, w_down)
    side = lax.axis_index("dp").astype(jnp.int32).reshape(1)
    order = Order()

    sources = {"own": (acts, cotangent)}

    def gather(block, origin, bit):
        sources[block] = tuple(from_partner(array, "grid", bit) for array in sources[origin])

    gather("near", "own", near)
    gather("far", "own", far)

    a = max(1, n_tiles * 4 // 7)
    every = (0, n_tiles)
    chunks = {"c0": (0, a), "c1": (a, n_tiles - a)}
    own, ready, got, pairs = {}, {}, {}, {}

    def compute(names, units, tiles, block, pack=False):
        results, pair = partials(order, units, tiles, sources[block], weights, pack=pack)
        for name, (kept, rounded) in zip(names, results):
            own[name], ready[name] = kept, rounded
        if pack:
            pairs[block] = order.need(both_replicas(pair), 0)

    def send(name, after=()):
        rounded = ready[name]
        if after:
            rounded = order.hold(rounded, [got[key] for key in after])
        got[name] = from_partner(rounded, "grid", across)

    hqr, sums = {}, {}

    def both_replicas(pair):
        return lax.all_to_all(pair, "dp", 0, 0, tiled=True)

    def finish(name, tiles, parts=None, addend=(), calls=99, cuts=None):
        parts = [(own[key], got[key]) for key in parts or [name]]
        out_type = jnp.bfloat16 if tiles == every else jnp.float32
        twice = name not in ("fa", "fb")
        found, *rest = hidden_and_back(
            order, tiles, parts, weights, out_type, addend, cuts, twice
        )
        if twice:
            hqr[name] = (order.need(both_replicas(found), calls),)
        else:
            for cut, part in enumerate((found, rest.pop(0))):
                hqr[name, cut] = (part, order.need(from_partner(part, "dp", 0), calls))
        sums[name] = rest

    def pieces_of(*groups):
        found = []
        at = 0
        for group in groups:
            size = sum(hqr[names[0]][0].shape[2] for names in group)
            for names in group:
                found.append((at, at + size, *(array for name in names for array in hqr[name])))
                at += hqr[names[0]][0].shape[2]
            at += size
        return found

    def pass_on(array, bit, calls):
        return order.need(from_partner(array, "grid", bit), calls)

    def collect(*names):
        return assemble(order, [pairs[name] for name in names])

    gup = (G, U, PRE)
    everything = [(gup, 0, rows)]
    halves = [(gup, 0, half), (gup, half, half)]
    compute(["c0"], everything, chunks["c0"], "own")
    send("c0")
    compute(["c1"], everything, chunks["c1"], "own", pack=True)
    compute(["near"], everything, every, "near", pack=True)
    send("near")
    finish("c0", chunks["c0"], calls=1)
    sources["far"] = tuple(order.hold(array, []) for array in sources["far"])
    gather("both", "far", near)
    compute(["fa", "fb"], halves, every, "far", pack=True)
    send("c1", ["c0"])
    early = collect("near", "own")
    compute(["ba", "bb"], halves, every, "both", pack=True)
    send("ba")
    late = collect("both", "far")
    send("bb", ["near"])
    finish("near", every, calls=0, cuts=[half] * 2)
    near_sums = [pass_on(array, near, 3) for array in sums["near"]]
    early_pieces = pieces_of([["near"]], [["c0"]])
    first = weight_grads(order, side, chunks["c0"], early, early_pieces, width)
    finish("c1", chunks["c1"], addend=sums["c0"], calls=0)
    early_pieces = pieces_of([["near"]], [["c0", "c1"]])
    send("fa", ["ba", "bb"])
    finish("both", every, parts=["ba", "bb"], calls=3, cuts=[half // 2] * 2 + [half])
    send("fb", ["bb"])
    *leading, trailing = sums["both"]
    both_sums = [[pass_on(array, near, 99) for array in leading]]
    first = weight_grads(order, side, chunks["c1"], early, early_pieces, width, into=first)
    both_sums.append([pass_on(order.hold(trailing, []), near, 99)])
    far_sums = []
    for name, addend in zip(("fa", "fb"), both_sums):
        finish(name, every, addend=addend, calls=0)
        far_sums.append(pass_on(sums[name][0], far, 99))
    far_names = [[(name, cut)] for name in ("fa", "fb") for cut in range(2)]
    late_pieces = pieces_of([["both"]], far_names)
    grads = weight_grads(order, side, every, late, late_pieces, width, first)
    outs = add_row_sums(order, sums["c1"][0], near_sums, far_sums, acts, cotangent)
    return (*outs, *grads)


def per_device(acts, cotangent, w_gate, w_up, w_down):
    fits = acts.shape[2] % 64 == 0 and acts.shape[3] % TILE == 0 and w_gate.shape[2] % TILE == 0
    if lax.axis_size("grid") == 8 and lax.axis_size("dp") == 2 and fits:
        return two_by_four(acts, cotangent, w_gate, w_up, w_down)
    return any_grid(acts, cotangent, w_gate, w_up, w_down)


def solution(mesh):
    return jax.shard_map(
        per_device,
        mesh=mesh,
        in_specs=(
            P(("groups", "dp"), "grid", None, None),
            P(("groups", "dp"), "grid", None, None),
            P("grid", None, None),
            P("grid", None, None),
            P("grid", None, None),
        ),
        out_specs=(
            P(("groups", "dp"), "grid", None, None),
            P(("groups", "dp"), "grid", None, None),
            P(("groups", "grid"), None, None),
            P(("groups", "grid"), None, None),
            P(("groups", "grid"), None, None),
        ),
        check_vma=False,
    )
```

```python
import functools
import itertools

import jax
import jax.numpy as jnp
from jax import lax
from jax.experimental import pallas as pl
from jax.experimental.pallas import tpu as pltpu
from jax.sharding import PartitionSpec as P

VMEM_BYTES = 62 * 1024 * 1024
TILE = 256
COST_SCALE = 0.2e9
G, U, PRE = 0, 1, 2


def from_partner(block, axis, stride):
    count = lax.axis_size(axis)
    route = []
    for low in range(count):
        high = low | 1 << stride
        if high != low and high < count:
            route += [(low, high), (high, low)]
    return lax.ppermute(block, axis, route)


def contract_rows(left, right):
    return lax.dot_general(
        left, right, (((0,), (0,)), ((), ())), preferred_element_type=jnp.float32
    )


def contract_cols(left, right):
    return lax.dot_general(
        left, right, (((1,), (1,)), ((), ())), preferred_element_type=jnp.float32
    )


def order_pair(is_upper, mine, other, dim=1):
    return jnp.where(
        is_upper, jnp.concatenate([other, mine], dim), jnp.concatenate([mine, other], dim)
    )


def column_sum(partial_term, total_rows, col_bits, row_bits, my_row):
    result_sum = partial_term(0, total_rows)
    for level_bit in range(row_bits - 1, -1, -1):
        half_rows = result_sum.shape[1] // 2
        lower_half = result_sum[:, :half_rows]
        upper_half = result_sum[:, half_rows:]
        is_upper = my_row >> level_bit & 1 == 1
        kept_half = jnp.where(is_upper, upper_half, lower_half)
        given_half = jnp.where(is_upper, lower_half, upper_half)
        result_sum = kept_half + from_partner(
            given_half.astype(jnp.bfloat16), "grid", col_bits + level_bit
        ).astype(given_half.dtype)
    return result_sum


def column_gather(pieces, col_bits, row_bits, my_row):
    for level_bit in range(row_bits):
        partner = from_partner(pieces, "grid", col_bits + level_bit)
        pieces = order_pair(my_row >> level_bit & 1 == 1, pieces, partner)
    return pieces


def row_sum(full_sum, col_bits, my_col):
    for level_bit in range(col_bits - 1, -1, -1):
        half_rows = full_sum.shape[0] // 2
        lower_half = full_sum[:half_rows]
        upper_half = full_sum[half_rows:]
        is_upper = my_col >> level_bit & 1 == 1
        kept_half = jnp.where(is_upper, upper_half, lower_half)
        given_half = jnp.where(is_upper, lower_half, upper_half)
        full_sum = kept_half + from_partner(
            given_half.astype(jnp.bfloat16), "grid", level_bit
        ).astype(given_half.dtype)
    return full_sum


def any_grid(acts, cotangent, w_gate, w_up, w_down):
    grid_size = lax.axis_size("grid")
    grid_cols = min(8, grid_size // 2)
    grid_rows = grid_size // grid_cols
    col_bits = grid_cols.bit_length() - 1
    row_bits = grid_rows.bit_length() - 1
    position = lax.axis_index("grid")
    my_row = position // grid_cols
    my_col = position % grid_cols
    own_acts = acts[0, 0]
    own_grads = cotangent[0, 0]
    gate_tile = w_gate[0]
    up_tile = w_up[0]
    down_tile = w_down[0]
    gathered = jnp.stack([own_acts, own_grads])
    for level_bit in range(col_bits):
        partner = from_partner(gathered, "grid", level_bit)
        gathered = order_pair(my_col >> level_bit & 1 == 1, gathered, partner)
    inputs_row = gathered[0]
    out_grad_row = gathered[1]
    total_rows = inputs_row.shape[0]

    def gate_up_term(row_start, row_count):
        return jnp.stack(
            [
                jnp.dot(inputs_row, gate_tile, preferred_element_type=jnp.float32),
                jnp.dot(inputs_row, up_tile, preferred_element_type=jnp.float32),
            ]
        )

    summed = column_sum(gate_up_term, total_rows, col_bits, row_bits, my_row)
    gate_pre = summed[0]
    up_proj = summed[1]
    sigmoid_g = jax.nn.sigmoid(gate_pre)
    activated = gate_pre * sigmoid_g
    hidden = (activated * up_proj).astype(jnp.bfloat16)
    hidden_full = column_gather(hidden[None], col_bits, row_bits, my_row)[0]
    output_sum = row_sum(
        jnp.dot(hidden_full, down_tile, preferred_element_type=jnp.float32), col_bits, my_col
    )
    block_out = (own_acts.astype(jnp.float32) + output_sum).astype(jnp.bfloat16)

    def hidden_grad_term(row_start, row_count):
        return contract_cols(out_grad_row, down_tile)[None]

    hidden_grad = column_sum(hidden_grad_term, total_rows, col_bits, row_bits, my_row)[0]
    gate_back = (hidden_grad * up_proj * sigmoid_g * (1.0 + gate_pre * (1.0 - sigmoid_g))).astype(
        jnp.bfloat16
    )
    up_back = (hidden_grad * activated).astype(jnp.bfloat16)
    backs_full = column_gather(jnp.stack([gate_back, up_back]), col_bits, row_bits, my_row)
    down_local = contract_rows(hidden_full, out_grad_row)
    input_part = contract_cols(backs_full[0], gate_tile) + contract_cols(backs_full[1], up_tile)
    input_sum = row_sum(input_part, col_bits, my_col)
    input_grad = (own_grads.astype(jnp.float32) + input_sum).astype(jnp.bfloat16)
    gate_local = contract_rows(inputs_row, backs_full[0])
    up_local = contract_rows(inputs_row, backs_full[1])
    gate_total, up_total, down_total = (
        lax.psum(gate_local.astype(jnp.bfloat16), "dp").astype(jnp.float32),
        lax.psum(up_local.astype(jnp.bfloat16), "dp").astype(jnp.float32),
        lax.psum(down_local.astype(jnp.bfloat16), "dp").astype(jnp.float32),
    )
    return (
        block_out[None, None],
        input_grad[None, None],
        gate_total.astype(jnp.bfloat16)[None],
        up_total.astype(jnp.bfloat16)[None],
        down_total.astype(jnp.bfloat16)[None],
    )


class Order:
    def __init__(self):
        self.token = None
        self.calls = 0
        self.due = []

    def need(self, array, calls):
        self.due.append((self.calls + calls, array))
        return array

    def call(self, body, name, cost, steps, inputs, outputs, scratch=(), after=(), aliases=()):
        after = list(after) + ([] if self.token is None else [self.token])
        after += [array for call, array in self.due if call <= self.calls]
        self.due = [(call, array) for call, array in self.due if call > self.calls]
        self.calls += 1
        n_in, n_after, n_out = len(inputs), len(after), len(outputs)

        def kernel(*refs):
            ins = refs[:n_in]
            outs = refs[n_in + n_after : n_in + n_after + n_out]
            refs[n_in + n_after + n_out][...] = jnp.zeros((8, 128), jnp.float32)
            body(ins, outs, refs[n_in + n_after + n_out + 1 :])

        *results, self.token = pl.pallas_call(
            kernel,
            name=name,
            grid=(steps,),
            in_specs=[spec for _, spec in inputs]
            + [pl.BlockSpec(memory_space=pl.ANY) for _ in after],
            out_specs=[spec for _, spec in outputs] + [pl.BlockSpec((8, 128), lambda j: (0, 0))],
            out_shape=[shape for shape, _ in outputs]
            + [jax.ShapeDtypeStruct((8, 128), jnp.float32)],
            scratch_shapes=list(scratch),
            input_output_aliases=dict(aliases),
            cost_estimate=pl.CostEstimate(
                flops=int(cost * COST_SCALE), bytes_accessed=0, transcendentals=0
            ),
            compiler_params=pltpu.CompilerParams(vmem_limit_bytes=VMEM_BYTES),
        )(*[array for array, _ in inputs], *after)
        return results

    def hold(self, array, after):
        inputs = [(array, pl.BlockSpec(memory_space=pl.ANY))]
        outputs = [(jax.ShapeDtypeStruct(array.shape, array.dtype), inputs[0][1])]
        return self.call(
            lambda *_: None, "hold", 0.6, 1, inputs, outputs, after=after, aliases={0: 0}.items()
        )[0]


def weight_specs(weights, kinds, first, tile=TILE):
    gate, up, down = weights
    depth = gate.shape[1]
    wide = pl.BlockSpec((1, depth, tile), lambda j: (0, 0, first + j))
    tall = pl.BlockSpec((1, tile, depth), lambda j: (0, first + j, 0))
    return [((gate, up, down)[kind], tall if kind == PRE else wide) for kind in kinds]


def partials(order, units, tiles, sources, weights, after=(), pack=False):
    first, count = tiles
    rows, depth = sources[0].shape[2:]
    kinds = [kind for kind in (G, U, PRE) if any(kind in unit[0] for unit in units)]
    token_spec = pl.BlockSpec((1, 1, rows, depth), lambda j: (0, 0, 0, 0))
    inputs = [(sources[kind == PRE], token_spec) for kind in kinds]
    inputs += weight_specs(weights, kinds, first)
    n = len(kinds)

    def body(ins, outs, _):
        for i, kind in enumerate(kinds):
            left, right = ins[i][0, 0], ins[n + i][0]
            if kind == PRE:
                term = contract_cols(left, right)
            else:
                term = jnp.dot(left, right, preferred_element_type=jnp.float32)
            for m, (unit_kinds, start, size) in enumerate(units):
                if kind in unit_kinds:
                    at = unit_kinds.index(kind)
                    outs[2 * m][at] = term[start : start + size]
                    outs[2 * m + 1][at] = term[start : start + size].astype(jnp.bfloat16)
        if pack:

            @pl.when(pl.program_id(0) == 0)
            def _():
                for d in range(2):
                    outs[-1][d, 0] = ins[kinds.index(G)][0, 0]
                    outs[-1][d, 1] = ins[kinds.index(PRE)][0, 0]

    outputs = []
    for unit_kinds, _, size in units:
        shape = (len(unit_kinds), size, count * TILE)
        spec = pl.BlockSpec((len(unit_kinds), size, TILE), lambda j: (0, 0, j))
        outputs.append((jax.ShapeDtypeStruct(shape, jnp.float32), spec))
        outputs.append((jax.ShapeDtypeStruct(shape, jnp.bfloat16), spec))
    if pack:
        shape = (2, 2, rows, depth)
        spec = pl.BlockSpec(shape, lambda j: (0, 0, 0, 0))
        outputs.append((jax.ShapeDtypeStruct(shape, jnp.bfloat16), spec))
    cost = (1 + 0.8 * count) * n
    results = order.call(body, "partials", cost, count, inputs, outputs, after=after)
    pairs = list(zip(results[: 2 * len(units) : 2], results[1::2]))
    return pairs, results[-1]


def hidden_and_back(order, tiles, parts, weights, out_type, addend=(), cuts=None, twice=True):
    first, count = tiles
    copies, hqr_cuts = (2, 1) if twice else (1, 2)
    tile = TILE
    if not twice and count % 2 == 1 and count * TILE % 256 == 0:
        tile, count = count * TILE // 2, 2
    sizes = [kept.shape[1] for kept, _ in parts]
    rows = sum(sizes)
    depth = weights[0].shape[1]
    inputs = []
    for pair, size in zip(parts, sizes):
        spec = pl.BlockSpec((3, size, tile), lambda j: (0, 0, j))
        inputs += [(array, spec) for array in pair]
    n = len(inputs)
    size = rows // hqr_cuts
    inputs += weight_specs(weights, (G, U, PRE), first, tile)
    inputs += [(array, pl.BlockSpec(array.shape, lambda j: (0, 0, 0))) for array in addend]
    cuts = cuts or [rows]

    def body(ins, outs, scratch):
        wg_ref, wu_ref, wd_ref = ins[n : n + 3]
        acc_ref = scratch[0]
        j = pl.program_id(0)
        terms = [ins[m][...] + ins[m + 1][...].astype(jnp.float32) for m in range(0, n, 2)]
        g, u, p = terms[0] if len(terms) == 1 else jnp.concatenate(terms, 1)
        s = jax.nn.sigmoid(g)
        a = g * s
        h = (a * u).astype(jnp.bfloat16)
        q = (p * u * s * (1.0 + g * (1.0 - s))).astype(jnp.bfloat16)
        r = (p * a).astype(jnp.bfloat16)
        for i, value in enumerate((h, q, r)):
            for cut, copy in itertools.product(range(hqr_cuts), range(copies)):
                outs[cut][copy, i] = value[cut * size : (cut + 1) * size]
        out_term = jnp.dot(h, wd_ref[0], preferred_element_type=jnp.float32)
        in_term = contract_cols(q, wg_ref[0]) + contract_cols(r, wu_ref[0])

        @pl.when(j == 0)
        def _():
            acc_ref[0] = out_term
            acc_ref[1] = in_term

        @pl.when(j > 0)
        def _():
            acc_ref[0] += out_term
            acc_ref[1] += in_term

        @pl.when(j == count - 1)
        def _():
            at = 0
            for ref in ins[n + 3 :]:
                acc_ref[:, at : at + ref.shape[1]] += ref[...].astype(jnp.float32)
                at += ref.shape[1]
            at = 0
            for ref in outs[hqr_cuts:]:
                ref[...] = acc_ref[:, at : at + ref.shape[1]].astype(out_type)
                at += ref.shape[1]

    outputs = [
        (
            jax.ShapeDtypeStruct((copies, 3, size, count * tile), jnp.bfloat16),
            pl.BlockSpec((copies, 3, size, tile), lambda j: (0, 0, 0, j)),
        )
    ] * hqr_cuts
    for cut in cuts:
        shape = (2, cut, depth)
        spec = pl.BlockSpec(shape, lambda j: (0, 0, 0))
        outputs.append((jax.ShapeDtypeStruct(shape, out_type), spec))
    scratch = [pltpu.VMEM((2, rows, depth), jnp.float32)]
    return order.call(body, "hidden_and_back", 3 + 2.2 * count * tile // TILE, count, inputs, outputs, scratch)


def assemble(order, blocks):
    n = len(blocks)
    rows, depth = blocks[0].shape[2:]
    total = 2 * rows * n
    inputs = []
    for block in blocks:
        for part in range(2):
            index = functools.partial(lambda j, part: (0, part, 0, j), part=part)
            inputs.append((block, pl.BlockSpec((2, 1, rows, TILE), index)))

    def body(ins, outs, scratch):
        xt_ref, e_ref = outs
        x_all = scratch[0]
        for b in range(n):
            for d in range(2):
                at = pl.ds((2 * b + d) * rows, rows)
                x_all[at, :] = ins[2 * b][d, 0]
                e_ref[at, :] = ins[2 * b + 1][d, 0]
        xt_ref[...] = x_all[...].T

    outputs = [
        (
            jax.ShapeDtypeStruct((depth, total), jnp.bfloat16),
            pl.BlockSpec((TILE, total), lambda j: (j, 0)),
        ),
        (
            jax.ShapeDtypeStruct((total, depth), jnp.bfloat16),
            pl.BlockSpec((total, TILE), lambda j: (0, j)),
        ),
    ]
    scratch = [pltpu.VMEM((total, TILE), jnp.bfloat16)]
    return order.call(body, "assemble", 5 * n, depth // TILE, inputs, outputs, scratch)


def weight_grads(order, side, tiles, tokens, pieces, width, so_far=None, into=None):
    first, count = tiles
    xt, e_all = tokens
    depth, total = xt.shape
    whole = [
        pl.BlockSpec((depth, total), lambda j: (0, 0), pipeline_mode=pl.Buffered(1)),
        pl.BlockSpec((total, depth), lambda j: (0, 0), pipeline_mode=pl.Buffered(1)),
    ]
    inputs = [(side, pl.BlockSpec(memory_space=pltpu.SMEM)), (xt, whole[0]), (e_all, whole[1])]
    bounds = []
    for _, _, *arrays in pieces:
        at = 0
        for hqr in arrays:
            at = 0 if hqr.shape[0] == 1 else at
            size = hqr.shape[3] // TILE

            def index(j, at, size):
                return 0, 0, 0, jnp.clip(first + j - at, 0, size - 1)

            spec = pl.BlockSpec(
                (hqr.shape[0], 3, hqr.shape[2], TILE),
                functools.partial(index, at=at, size=size),
            )
            inputs.append((hqr, spec))
            bounds.append((at, at + size))
            at += size
    wide = pl.BlockSpec((1, depth, TILE), lambda j: (0, 0, first + j))
    tall = pl.BlockSpec((1, TILE, depth), lambda j: (0, first + j, 0))
    specs = (wide, wide, tall)
    n = len(inputs)
    if so_far is not None:
        inputs += list(zip(so_far, specs))
    aliases = {}
    if into is not None:
        for i, array in enumerate(into):
            aliases[len(inputs)] = i
            inputs.append((array, pl.BlockSpec(memory_space=pl.ANY)))

    def body(ins, outs, scratch):
        hqr_all = scratch[0]
        tile = first + pl.program_id(0)
        m = 0
        for lower, higher, *arrays in pieces:
            for n_array, hqr in enumerate(arrays):

                def take(m=m, starts=(lower, higher), rows=hqr.shape[2]):
                    for d, start in enumerate(starts):
                        for i in range(3):
                            hqr_all[i, pl.ds(start, rows), :] = ins[3 + m][d, i]

                if hqr.shape[0] == 1:
                    upper = ins[0][0] if n_array == 0 else 1 - ins[0][0]
                    start = pl.multiple_of(lower + upper * (higher - lower), 16)
                    take(starts=(start,))
                elif len(arrays) == 1:
                    take()
                else:
                    low, high = bounds[m]
                    pl.when((tile >= low) & (tile < high))(take)
                m += 1
        terms = (
            lambda: jnp.dot(ins[1][...], hqr_all[1], preferred_element_type=jnp.float32),
            lambda: jnp.dot(ins[1][...], hqr_all[2], preferred_element_type=jnp.float32),
            lambda: contract_rows(hqr_all[0], ins[2][...]),
        )
        for i, term in enumerate(terms):
            value = term()
            if so_far is not None:
                value = value + ins[n + i][0].astype(jnp.float32)
            outs[i][0] = value.astype(jnp.bfloat16)

    shapes = ((1, depth, width), (1, depth, width), (1, width, depth))
    outputs = [
        (jax.ShapeDtypeStruct(shape, jnp.bfloat16), spec) for shape, spec in zip(shapes, specs)
    ]
    scratch = [pltpu.VMEM((3, total, TILE), jnp.bfloat16)]
    return order.call(
        body, "weight_grads", 4 + 2 * count, count, inputs, outputs, scratch, aliases=aliases.items()
    )


def add_row_sums(order, own_sums, near_sums, far_sums, acts, cotangent):
    rows, depth = acts.shape[2:]
    cuts = len(far_sums)
    step = rows // cuts
    spec = pl.BlockSpec((2, step, depth), lambda j: (0, j, 0))
    each = pl.BlockSpec((2, step, depth), lambda j: (0, 0, 0))
    token_spec = pl.BlockSpec((1, 1, step, depth), lambda j: (0, 0, j, 0))
    inputs = [(own_sums, spec), (acts, token_spec), (cotangent, token_spec)]
    inputs += [(array, each) for array in (*near_sums, *far_sums)]

    def body(ins, outs, _):
        def add(j):
            for i in range(2):
                total = ins[0][i] + ins[3 + j][i].astype(jnp.float32)
                total += ins[3 + cuts + j][i].astype(jnp.float32)
                total += ins[1 + i][0, 0].astype(jnp.float32)
                outs[i][0, 0] = total.astype(jnp.bfloat16)

        for j in range(cuts):
            pl.when(pl.program_id(0) == j)(functools.partial(add, j))

    outputs = [(jax.ShapeDtypeStruct(acts.shape, jnp.bfloat16), token_spec)] * 2
    return order.call(body, "add_row_sums", 5, cuts, inputs, outputs)


def two_by_four(acts, cotangent, w_gate, w_up, w_down):
    near, far, across = 0, 1, 2
    rows = acts.shape[2]
    half = rows // 2
    width = w_gate.shape[2]
    n_tiles = width // TILE
    weights = (w_gate, w_up, w_down)
    side = lax.axis_index("dp").astype(jnp.int32).reshape(1)
    order = Order()

    sources = {"own": (acts, cotangent)}

    def gather(block, origin, bit):
        sources[block] = tuple(from_partner(array, "grid", bit) for array in sources[origin])

    gather("near", "own", near)
    gather("far", "own", far)

    a = max(1, n_tiles * 4 // 7)
    every = (0, n_tiles)
    chunks = {"c0": (0, a), "c1": (a, n_tiles - a)}
    own, ready, got, pairs = {}, {}, {}, {}

    def compute(names, units, tiles, block, pack=False):
        results, pair = partials(order, units, tiles, sources[block], weights, pack=pack)
        for name, (kept, rounded) in zip(names, results):
            own[name], ready[name] = kept, rounded
        if pack:
            pairs[block] = order.need(both_replicas(pair), 0)

    def send(name, after=()):
        rounded = ready[name]
        if after:
            rounded = order.hold(rounded, [got[key] for key in after])
        got[name] = from_partner(rounded, "grid", across)

    hqr, sums = {}, {}

    def both_replicas(pair):
        return lax.all_to_all(pair, "dp", 0, 0, tiled=True)

    def finish(name, tiles, parts=None, addend=(), calls=99, cuts=None):
        parts = [(own[key], got[key]) for key in parts or [name]]
        out_type = jnp.bfloat16 if tiles == every else jnp.float32
        twice = name not in ("fa", "fb")
        found, *rest = hidden_and_back(
            order, tiles, parts, weights, out_type, addend, cuts, twice
        )
        if twice:
            hqr[name] = (order.need(both_replicas(found), calls),)
        else:
            for cut, part in enumerate((found, rest.pop(0))):
                hqr[name, cut] = (part, order.need(from_partner(part, "dp", 0), calls))
        sums[name] = rest

    def pieces_of(*groups):
        found = []
        at = 0
        for group in groups:
            size = sum(hqr[names[0]][0].shape[2] for names in group)
            for names in group:
                found.append((at, at + size, *(array for name in names for array in hqr[name])))
                at += hqr[names[0]][0].shape[2]
            at += size
        return found

    def pass_on(array, bit, calls):
        return order.need(from_partner(array, "grid", bit), calls)

    def collect(*names):
        return assemble(order, [pairs[name] for name in names])

    gup = (G, U, PRE)
    everything = [(gup, 0, rows)]
    halves = [(gup, 0, half), (gup, half, half)]
    compute(["c0"], everything, chunks["c0"], "own")
    send("c0")
    compute(["c1"], everything, chunks["c1"], "own", pack=True)
    compute(["near"], everything, every, "near", pack=True)
    send("near")
    finish("c0", chunks["c0"], calls=1)
    sources["far"] = tuple(order.hold(array, []) for array in sources["far"])
    gather("both", "far", near)
    compute(["fa", "fb"], halves, every, "far", pack=True)
    send("c1", ["c0"])
    early = collect("near", "own")
    compute(["ba", "bb"], halves, every, "both", pack=True)
    send("ba")
    late = collect("both", "far")
    send("bb", ["near"])
    finish("near", every, calls=0, cuts=[half] * 2)
    near_sums = [pass_on(array, near, 3) for array in sums["near"]]
    early_pieces = pieces_of([["near"]], [["c0"]])
    first = weight_grads(order, side, chunks["c0"], early, early_pieces, width)
    finish("c1", chunks["c1"], addend=sums["c0"], calls=0)
    early_pieces = pieces_of([["near"]], [["c0", "c1"]])
    send("fa", ["ba", "bb"])
    finish("both", every, parts=["ba", "bb"], calls=3, cuts=[half // 2] * 2 + [half])
    *leading, trailing = sums["both"]
    both_sums = [[pass_on(array, near, 99) for array in leading]]
    first = weight_grads(order, side, chunks["c1"], early, early_pieces, width, into=first)
    send("fb", ["bb"])
    both_sums.append([pass_on(order.hold(trailing, []), near, 99)])
    far_sums = []
    for name, addend in zip(("fa", "fb"), both_sums):
        finish(name, every, addend=addend, calls=0)
        far_sums.append(pass_on(sums[name][0], far, 99))
    far_names = [[(name, cut)] for name in ("fa", "fb") for cut in range(2)]
    late_pieces = pieces_of([["both"]], far_names)
    grads = weight_grads(order, side, every, late, late_pieces, width, first)
    outs = add_row_sums(order, sums["c1"][0], near_sums, far_sums, acts, cotangent)
    return (*outs, *grads)


def per_device(acts, cotangent, w_gate, w_up, w_down):
    fits = acts.shape[2] % 64 == 0 and acts.shape[3] % TILE == 0 and w_gate.shape[2] % TILE == 0
    if lax.axis_size("grid") == 8 and lax.axis_size("dp") == 2 and fits:
        return two_by_four(acts, cotangent, w_gate, w_up, w_down)
    return any_grid(acts, cotangent, w_gate, w_up, w_down)


def solution(mesh):
    return jax.shard_map(
        per_device,
        mesh=mesh,
        in_specs=(
            P(("groups", "dp"), "grid", None, None),
            P(("groups", "dp"), "grid", None, None),
            P("grid", None, None),
            P("grid", None, None),
            P("grid", None, None),
        ),
        out_specs=(
            P(("groups", "dp"), "grid", None, None),
            P(("groups", "dp"), "grid", None, None),
            P(("groups", "grid"), None, None),
            P(("groups", "grid"), None, None),
            P(("groups", "grid"), None, None),
        ),
        check_vma=False,
    )
```
